256 devices in a mesh: lender: 32 (over y, z), tensor: 8 (over x, core).
Axes of the slice: x: 4, y: 4, z: 8, core: 2. Of those that a mesh axis runs over, the one named last changes fastest.
Arguments:
- draft_queries: bfloat16 [64, 4, 128, 192], P('lender', None, 'tensor'), may hold values from -6.5 to 6.5
- draft_latents: bfloat16 [64, 4, 576], P('lender'), may hold values from -15 to 15
- latent_pool: bfloat16 [1024, 192, 576], P('lender'), may hold values from -6 to 6
- key_absorb: bfloat16 [128, 128, 512], P('tensor'), may hold values from -0.5 to 0.5
- value_absorb: bfloat16 [128, 512, 128], P('tensor'), may hold values from -0.25 to 0.25
- out_proj: bfloat16 [16384, 7168], P('tensor', 'lender'), may hold values from -0.046875 to 0.046875
- slot_request: int32 [32, 32], replicated, may hold values from 0 to 63, as said below
- context_lengths: int32 [64], replicated, may hold values from 1 to 5952, as said below
Outputs:
- mixed: bfloat16 [64, 4, 7168], P('tensor', None, 'lender')
The draws below stay inside these ranges and needn't reach their ends.
Inputs may be any that keep to these rules, and one draw needn't show every extreme that they name: slot_request[d, e] lies in e * 2 to (e + 1) * 2 - 1, and every request holds at least one slot. With n slots holding request r, context_lengths[r] lies in 192 (n - 1) + 1 to 192 n; the maximum 192 (31) is reached in every draw.
All inputs are finite; a program needn't handle non-finite values.
Results may differ from the reference program's by a relative error of at most 0.02.
Values may be sent and summed in bfloat16 or wider, within the bound.
No kernel may reach another device: no remote copies, remote signals or barrier semaphores. Data moves between devices by JAX's collectives and lax.ppermute only.
A program may use at most 64 MiB of HBM per device.

```python
import math
import jax
import jax.numpy as jnp
from jax import lax

D = 7168
HEADS = 128
NOPE = 128
ROPE = 64
LATENT = 512
VHEAD = 128
DRAFTS = 4
SLOT_TOKENS = 192
REQ_DEV = 2
REQUESTS = 64
SLOTS = 1024
N_LENDER = 32


def lending_plan(key):
    key = jax.random.fold_in(key, 7)
    key_order, key_first, key_second, key_tail, key_heavy = jax.random.split(key, 5)
    lender_ids = jnp.arange(N_LENDER, dtype=jnp.int32)
    priority = jax.random.randint(key_order, (N_LENDER, N_LENDER), 0, 1 << 20) * N_LENDER + lender_ids[:, None]
    position = jnp.argsort(jnp.argsort(priority, axis=0), axis=0).astype(jnp.int32)
    first = jax.random.randint(key_first, (N_LENDER, N_LENDER), 0, REQ_DEV)
    second = jax.random.randint(key_second, (N_LENDER, N_LENDER), 0, REQ_DEV)
    heavy_pick = jax.random.randint(key_heavy, (2,), 0, 1 << 20)
    heavy_home = heavy_pick[0] % N_LENDER
    heavy_local = heavy_pick[1] % REQ_DEV
    extra_index = jnp.where(lender_ids[None, :] == heavy_home, heavy_local, jnp.minimum(first, second))
    local_index = jnp.where(position < REQ_DEV, position, extra_index)
    slots = lender_ids[None, :] * REQ_DEV + local_index
    owners = jnp.arange(REQUESTS, dtype=jnp.int32)
    held = jnp.sum(jnp.where(slots[:, :, None] == owners[None, None, :], 1, 0), axis=(0, 1))
    tail = jax.random.randint(key_tail, (REQUESTS,), 1, SLOT_TOKENS + 1)
    tail = jnp.where(owners == heavy_home * REQ_DEV + heavy_local, SLOT_TOKENS, tail)
    lengths = SLOT_TOKENS * (held - 1) + tail
    return (slots.astype(jnp.int32), lengths.astype(jnp.int32))


def draw_slot_request(key, part):
    return lending_plan(key)[0]


def draw_context_lengths(key, part):
    return lending_plan(key)[1]


def draw_latent_pool(key, part):
    key = jax.random.fold_in(key, 1)
    key_main = jax.random.fold_in(key, 0)
    full = jnp.clip(jax.random.normal(key_main, (SLOTS, SLOT_TOKENS, LATENT + ROPE)), -6.0, 6.0)
    return full.astype(jnp.bfloat16)


def draw_draft_queries(key, part):
    key = jax.random.fold_in(key, 2)
    key_main = jax.random.fold_in(key, 0)
    full = jnp.clip(jax.random.normal(key_main, (REQUESTS, DRAFTS, HEADS, NOPE + ROPE)), -6.0, 6.0)
    return full.astype(jnp.bfloat16)


def draw_draft_latents(key, part):
    key = jax.random.fold_in(key, 3)
    key_main = jax.random.fold_in(key, 0)
    full = jnp.clip(2.5 * jax.random.normal(key_main, (REQUESTS, DRAFTS, LATENT + ROPE)), -15.0, 15.0)
    return full.astype(jnp.bfloat16)


def level_of(key, dims, shards, low, largest):
    def one(axis_at, parts):
        steps = jax.random.uniform(jax.random.fold_in(jax.random.fold_in(key, 6), axis_at), (parts,), jnp.float32, low / len(shards), largest / len(shards))
        return jnp.repeat(jnp.exp(steps), dims[axis_at] // parts).reshape((-1,) + (1,) * (len(dims) - axis_at - 1))

    level = one(*shards[0])
    for cut in shards[1:]:
        level = level * one(*cut)
    return level


def normal_values(stream_key, dims, width, limit, cuts=(), held_as=jnp.bfloat16):
    entries = jax.random.normal(stream_key, dims, jnp.float32) * width
    if len(cuts) > 0:
        entries = level_of(stream_key, dims, cuts, -0.22, 0.18) * entries
    return jnp.clip(entries, min=-limit, max=limit).astype(held_as)


def setup_inputs(seed: int = 0) -> dict:
    arg_keys = jax.random.split(jax.random.key(seed), 9)
    return {
        "draft_queries": draw_draft_queries(jax.random.fold_in(arg_keys[8], 71), 0),
        "draft_latents": draw_draft_latents(jax.random.fold_in(arg_keys[8], 71), 0),
        "latent_pool": draw_latent_pool(jax.random.fold_in(arg_keys[8], 71), 0),
        "key_absorb": normal_values(arg_keys[3], (HEADS, NOPE, LATENT), NOPE ** -0.5, 0.5, ((0, 8),)),
        "value_absorb": normal_values(arg_keys[4], (HEADS, LATENT, VHEAD), LATENT ** -0.5, 0.25, ((0, 8),)),
        "out_proj": normal_values(arg_keys[5], (HEADS * VHEAD, D), (HEADS * VHEAD) ** -0.5, 0.046875, ((0, 8), (1, 32))),
        "slot_request": draw_slot_request(jax.random.fold_in(arg_keys[8], 71), 0),
        "context_lengths": draw_context_lengths(jax.random.fold_in(arg_keys[8], 71), 0),
    }


MSCALE_SQ = (0.1 * math.log(40.0) + 1.0) ** 2
NEG_FILL = -1e30


def absorb(queries, key_absorb):
    latent_part = jnp.einsum("nshc,hcl->nshl", queries[..., :NOPE].astype(jnp.float32), key_absorb.astype(jnp.float32), precision=lax.Precision.HIGHEST)
    return jnp.concatenate([latent_part.astype(jnp.bfloat16), queries[..., NOPE:]], axis=-1)


def live_tokens(slot_request, context_lengths, slot_tokens):
    lenders = slot_request.shape[0]
    owners = jnp.arange(context_lengths.shape[0], dtype=jnp.int32)
    lengths = jnp.sum(jnp.where(slot_request[:, :, None] == owners[None, None, :], context_lengths[None, None, :], 0), axis=-1)
    matching = slot_request[:, None, :] == slot_request[None, :, :]
    before = jnp.arange(lenders)[:, None] < jnp.arange(lenders)[None, :]
    slot_rank = jnp.sum(jnp.where(matching & before[:, :, None], 1, 0), axis=0)
    return jnp.clip(lengths - slot_tokens * slot_rank, 0, slot_tokens).astype(jnp.int32)


def slot_partials(queries, blocks, live_here, score_scale):
    scores = jnp.einsum("nshk,ntk->nsht", queries.astype(jnp.float32), blocks.astype(jnp.float32), precision=lax.Precision.HIGHEST) * score_scale
    usable = jnp.arange(blocks.shape[1])[None, :] < live_here[:, None]
    scores = jnp.where(usable[:, None, None, :], scores, NEG_FILL)
    slot_top = jnp.max(scores, axis=-1)
    weights = jnp.exp(scores - slot_top[..., None])
    slot_total = jnp.sum(weights, axis=-1)
    weighted = jnp.einsum("nsht,ntl->nshl", weights.astype(jnp.bfloat16).astype(jnp.float32), blocks[:, :, :LATENT].astype(jnp.float32), precision=lax.Precision.HIGHEST)
    return (weighted / slot_total[..., None]).astype(jnp.bfloat16), slot_top, slot_total


def finish(numerator, denominator, slot_top, absorbed, drafts, value_absorb, score_scale):
    scores = jnp.einsum("ishk,ijk->ishj", absorbed.astype(jnp.float32), drafts.astype(jnp.float32), precision=lax.Precision.HIGHEST) * score_scale
    steps_count = drafts.shape[1]
    causal = jnp.arange(steps_count)[:, None] >= jnp.arange(steps_count)[None, :]
    scores = jnp.where(causal[None, :, None, :], scores, NEG_FILL)
    row_top = jnp.maximum(slot_top, jnp.max(scores, axis=-1))
    draft_weights = jnp.exp(scores - row_top[..., None])
    shrink = jnp.exp(slot_top - row_top)
    draft_values = jnp.einsum("ijl,hlc->ijhc", drafts[:, :, :LATENT].astype(jnp.float32), value_absorb.astype(jnp.float32), precision=lax.Precision.HIGHEST)
    full_num = numerator * shrink[..., None] + jnp.einsum("ishj,ijhc->ishc", draft_weights, draft_values, precision=lax.Precision.HIGHEST)
    full_den = denominator * shrink + jnp.sum(draft_weights, axis=-1)
    return (full_num / full_den[..., None]).astype(jnp.bfloat16)


def reference(draft_queries, draft_latents, latent_pool, key_absorb, value_absorb, out_proj, slot_request, context_lengths):
    score_scale = (NOPE + ROPE) ** -0.5 * MSCALE_SQ
    absorbed = absorb(draft_queries, key_absorb)
    live = live_tokens(slot_request, context_lengths, SLOT_TOKENS)
    pool_slots = latent_pool.reshape(N_LENDER, N_LENDER, SLOT_TOKENS, LATENT + ROPE)
    shape_rows = (REQUESTS, DRAFTS, HEADS)
    initial = (jnp.full(shape_rows, NEG_FILL, jnp.float32), jnp.zeros(shape_rows + (VHEAD,), jnp.float32), jnp.zeros(shape_rows, jnp.float32))
    value_wide = value_absorb.astype(jnp.float32)

    def visit_lender(carried, inputs):
        run_max, numerator, denominator = carried
        blocks, requests, live_here = inputs
        gathered = jnp.take(absorbed, requests, axis=0)
        slot_mean, slot_top, slot_total = slot_partials(gathered, blocks, live_here, score_scale)
        slot_value = jnp.einsum("nshl,hlc->nshc", slot_mean.astype(jnp.float32), value_wide, precision=lax.Precision.HIGHEST).astype(jnp.bfloat16)
        slot_max = jnp.full(shape_rows, NEG_FILL, jnp.float32).at[requests].max(slot_top)
        new_max = jnp.maximum(run_max, slot_max)
        factor = jnp.exp(run_max - new_max)
        weight = slot_total * jnp.exp(slot_top - jnp.take(new_max, requests, axis=0))
        numerator = numerator * factor[..., None] + jnp.zeros_like(numerator).at[requests].add(weight[..., None] * slot_value.astype(jnp.float32))
        denominator = denominator * factor + jnp.zeros_like(denominator).at[requests].add(weight)
        return (new_max, numerator, denominator), None

    (slot_top, numerator, denominator), _ = lax.scan(visit_lender, initial, (pool_slots, slot_request, live))
    heads_out = finish(numerator, denominator, slot_top, absorbed, draft_latents, value_absorb, score_scale)
    flattened = heads_out.reshape(REQUESTS, DRAFTS, HEADS * VHEAD)
    mixed = jnp.einsum("isc,cd->isd", flattened.astype(jnp.float32), out_proj.astype(jnp.float32), precision=lax.Precision.HIGHEST)
    return mixed.astype(jnp.bfloat16)
```

```python
import math

import jax
import jax.numpy as jnp
from jax import lax
from jax.sharding import PartitionSpec as P

MSCALE_SQ = (0.1 * math.log(40.0) + 1.0) ** 2
NEG_FILL = -1e30
BF16 = jnp.bfloat16
F32 = jnp.float32


def live_tokens(slot_request, context_lengths, slot_tokens):
    lenders = slot_request.shape[0]
    owners = jnp.arange(context_lengths.shape[0], dtype=jnp.int32)
    lengths = jnp.sum(
        jnp.where(
            slot_request[:, :, None] == owners[None, None, :], context_lengths[None, None, :], 0
        ),
        axis=-1,
    )
    matching = slot_request[:, None, :] == slot_request[None, :, :]
    before = jnp.arange(lenders)[:, None] < jnp.arange(lenders)[None, :]
    slot_rank = jnp.sum(jnp.where(matching & before[:, :, None], 1, 0), axis=0)
    return jnp.clip(lengths - slot_tokens * slot_rank, 0, slot_tokens)


def three_parts(x):
    high = lax.reduce_precision(x, 8, 7)
    rest = x - high
    middle = lax.reduce_precision(rest, 8, 7)
    return high.astype(BF16), middle.astype(BF16), (rest - middle).astype(BF16)


def body(
    draft_queries,
    draft_latents,
    latent_pool,
    key_absorb,
    value_absorb,
    out_proj,
    slot_request,
    context_lengths,
):
    home = lax.axis_index("lender")
    reqs, drafts, heads, width = draft_queries.shape
    nope, latent = key_absorb.shape[1:]
    rope = width - nope
    slots, tokens = latent_pool.shape[:2]
    vhead = value_absorb.shape[-1]
    rows = heads * drafts
    scale = width ** (-0.5) * MSCALE_SQ

    column = lax.dynamic_slice_in_dim(slot_request, home, 1, 1)[:, 0]
    local = column - home * reqs
    q = jnp.swapaxes(draft_queries, 1, 2).reshape(reqs, rows, width)
    q_rope = q[:, :, nope:]
    packed = jnp.concatenate(
        [q[:, :, :nope], jnp.concatenate([q_rope[:, : rows // 2], q_rope[:, rows // 2 :]], -1)], 1
    )
    outgoing = packed[0][None]
    for i in range(1, reqs):
        outgoing = jnp.where((local == i)[:, None, None], packed[i][None], outgoing)
    arrived = lax.all_to_all(outgoing, "lender", split_axis=0, concat_axis=0, tiled=True)

    def absorb(nope_part, rope_part):
        n = nope_part.shape[0]
        part = jnp.einsum(
            "nhsc,hcl->nhsl",
            nope_part.reshape(n, heads, drafts, nope),
            key_absorb,
            preferred_element_type=F32,
        ).astype(BF16)
        return jnp.concatenate([part.reshape(n, rows, latent), rope_part], -1)

    live_all = live_tokens(slot_request, context_lengths, tokens)
    live_here = lax.dynamic_slice_in_dim(live_all, home, 1, 0)[0]
    arrived_rope = arrived[:, rows:]
    queries = absorb(
        arrived[:, :rows],
        jnp.concatenate([arrived_rope[:, :, :rope], arrived_rope[:, :, rope:]], 1),
    )
    scores = jnp.einsum("nrk,ntk->nrt", queries, latent_pool, preferred_element_type=F32) * scale
    usable = jnp.arange(tokens)[None, :] < live_here[:, None]
    scores = jnp.where(usable[:, None, :], scores, NEG_FILL)
    top = jnp.max(scores, axis=-1)
    weights = jnp.exp(scores - top[..., None])
    total = jnp.sum(weights, axis=-1)
    weighted = jnp.einsum(
        "nrt,ntl->nrl",
        weights.astype(BF16),
        latent_pool[:, :, :latent],
        preferred_element_type=F32,
    )
    mean = (weighted / total[..., None]).astype(BF16)
    value = jnp.einsum(
        "nhsl,hlc->nhsc",
        mean.reshape(slots, heads, drafts, latent),
        value_absorb,
        preferred_element_type=F32,
    ).astype(BF16)
    mass = jnp.stack(three_parts(top + jnp.log(total)), axis=1)
    mass = jnp.pad(mass, ((0, 0), (0, 16 - 3), (0, vhead - rows)))
    sending = jnp.concatenate([value.reshape(slots, rows, vhead), mass], axis=1)
    back = lax.all_to_all(sending, "lender", split_axis=0, concat_axis=0, tiled=True)

    own = absorb(q[:, :, :nope], q_rope)
    draft_scores = (
        jnp.einsum("irk,ijk->irj", own, draft_latents, preferred_element_type=F32) * scale
    )
    causal = (jnp.arange(rows) % drafts)[:, None] >= jnp.arange(drafts)[None, :]
    draft_scores = jnp.where(causal[None], draft_scores, NEG_FILL)
    draft_values = jnp.einsum(
        "ijl,hlc->ijhc", draft_latents[:, :, :latent], value_absorb, preferred_element_type=F32
    )
    mass_back = jnp.sum(back[:, rows : rows + 3, :rows].astype(F32), axis=1)
    value_back = back[:, :rows].astype(F32)
    member = (local[:, None] == jnp.arange(reqs)[None, :])[:, :, None]
    mass_of = jnp.where(member, mass_back[:, None], NEG_FILL)
    row_top = jnp.maximum(jnp.max(mass_of, axis=0), jnp.max(draft_scores, axis=-1))
    weight = jnp.where(member, jnp.exp(mass_of - row_top[None]), 0.0)
    draft_weight = jnp.exp(draft_scores - row_top[..., None])
    numerator = jnp.sum(weight[..., None] * value_back[:, None], axis=0)
    numerator = numerator + jnp.sum(
        draft_weight.reshape(reqs, heads, drafts, drafts)[..., None]
        * jnp.swapaxes(draft_values, 1, 2)[:, :, None],
        axis=3,
    ).reshape(reqs, rows, vhead)
    denominator = jnp.sum(weight, axis=0) + jnp.sum(draft_weight, axis=-1)
    out = (numerator / denominator[..., None]).astype(BF16)
    out = jnp.swapaxes(out.reshape(reqs, heads, drafts, vhead), 1, 2)
    out = out.reshape(reqs * drafts, heads * vhead)

    copies = jnp.broadcast_to(out[None], (slots,) + out.shape)
    everyone = lax.all_to_all(copies, "lender", split_axis=0, concat_axis=0, tiled=True)
    partial = jnp.dot(
        everyone.reshape(-1, heads * vhead), out_proj, preferred_element_type=F32
    ).astype(BF16)
    parts = lax.axis_size("tensor")
    terms = lax.all_to_all(
        partial.reshape(parts, -1, partial.shape[-1]), "tensor", split_axis=0, concat_axis=0
    )
    mixed = jnp.sum(terms.astype(F32), axis=0).astype(BF16)
    return mixed.reshape(-1, drafts, partial.shape[-1])


def solution(mesh):
    in_specs = (
        P("lender", None, "tensor", None),
        P("lender", None, None),
        P("lender", None, None),
        P("tensor", None, None),
        P("tensor", None, None),
        P("tensor", "lender"),
        P(),
        P(),
    )
    out_specs = P("tensor", None, "lender")
    return jax.shard_map(body, mesh=mesh, in_specs=in_specs, out_specs=out_specs, check_vma=False)
```

```python
import functools
import math

import jax
import jax.numpy as jnp
from jax import lax
from jax.experimental import pallas as pl
from jax.experimental.pallas import tpu as pltpu
from jax.sharding import PartitionSpec as P

MSCALE_SQ = (0.1 * math.log(40.0) + 1.0) ** 2
NEG_FILL = -1e30
BF16 = jnp.bfloat16
F32 = jnp.float32
PARTS = 3


def live_tokens(slot_request, context_lengths, slot_tokens):
    lenders = slot_request.shape[0]
    owners = jnp.arange(context_lengths.shape[0], dtype=jnp.int32)
    lengths = jnp.sum(
        jnp.where(
            slot_request[:, :, None] == owners[None, None, :], context_lengths[None, None, :], 0
        ),
        axis=-1,
    )
    matching = slot_request[:, None, :] == slot_request[None, :, :]
    before = jnp.arange(lenders)[:, None] < jnp.arange(lenders)[None, :]
    slot_rank = jnp.sum(jnp.where(matching & before[:, :, None], 1, 0), axis=0)
    return jnp.clip(lengths - slot_tokens * slot_rank, 0, slot_tokens)


def pack_kernel(
    home_ref, slot_request_ref, queries_ref, out_ref, nope_ref, rope_ref, packed_ref, sems
):
    reqs, drafts, heads, width = queries_ref.shape
    nope = nope_ref.shape[-1]
    half = heads * drafts // 2
    for i in range(reqs):
        for s in range(drafts):
            x = queries_ref[i, s].astype(F32)
            nope_ref[pl.ds(s, heads, stride=drafts), :] = x[:, :nope]
            rope_ref[pl.ds(s, heads, stride=drafts), :] = x[:, nope:]
        rope = rope_ref[...]
        rope = jnp.concatenate([rope[:half], rope[half:]], 1)
        packed_ref[i] = jnp.concatenate([nope_ref[...], rope], 0).astype(BF16)
    home = home_ref[0]
    copies = [
        pltpu.make_async_copy(
            packed_ref.at[jnp.clip(slot_request_ref[d, home] - home * reqs, 0, reqs - 1)],
            out_ref.at[d],
            sems.at[d],
        )
        for d in range(out_ref.shape[0])
    ]
    for copy in copies:
        copy.start()
    for copy in copies:
        copy.wait()


def pack(home, slot_request, queries, nope):
    reqs, drafts, heads, width = queries.shape
    rows = heads * drafts
    smem = pl.BlockSpec(memory_space=pltpu.SMEM)
    vmem = pl.BlockSpec(memory_space=pltpu.VMEM)
    slots = slot_request.shape[0]
    return pl.pallas_call(
        pack_kernel,
        out_shape=pltpu.HBM((slots, rows + rows // 2, nope), BF16),
        in_specs=[smem, smem, vmem],
        out_specs=pl.BlockSpec(memory_space=pltpu.HBM),
        scratch_shapes=[
            pltpu.VMEM((rows, nope), F32),
            pltpu.VMEM((rows, width - nope), F32),
            pltpu.VMEM((reqs, rows + rows // 2, nope), BF16),
            pltpu.SemaphoreType.DMA((slots,)),
        ],
        name="pack",
    )(home, slot_request, queries)


def lend_kernel(
    scale,
    group,
    live_ref,
    arrived_any,
    keys_ref,
    values_any,
    pool_any,
    out_any,
    out_ref,
    arrived_ref,
    values_ref,
    pool_ref,
    query_ref,
    mean_ref,
    sems,
):
    slots, _, nope = arrived_ref.shape
    heads, _, latent = keys_ref.shape
    vhead = values_ref.shape[-1]
    rows, width = query_ref.shape[1:]
    drafts = rows // heads
    rope = width - latent
    tokens = pool_ref.shape[1]
    pair = 2 * drafts
    blocks = rows // 16
    trips = slots // group

    def arrival(b):
        at = pl.ds(16 * b, 16) if b < blocks else pl.ds(rows, rows // 2)
        return pltpu.make_async_copy(arrived_any.at[:, at], arrived_ref.at[:, at], sems.at[b])

    def pool_part(t):
        at = pl.ds(t * group, group)
        return pltpu.make_async_copy(pool_any.at[at], pool_ref.at[at], sems.at[blocks + 2 + t])

    def leaving(b):
        at = pl.ds(16 * b, 16)
        sem = sems.at[blocks + 2 + trips + b]
        return pltpu.make_async_copy(out_ref.at[:, at], out_any.at[:, at], sem)

    values_copy = pltpu.make_async_copy(values_any, values_ref, sems.at[blocks + 1])
    for b in range(blocks + 1):
        arrival(b).start()
    for t in range(trips):
        pool_part(t).start()
    values_copy.start()

    first = lax.broadcasted_iota(jnp.int32, (slots * pair, 1), 0) % pair < drafts

    for block in range(blocks):
        arrival(block).wait()
        part = arrived_ref[:, 16 * block : 16 * block + 16, :].astype(F32)
        done = []
        for half in range(16 // pair):
            rows_in = part[:, pair * half : pair * half + pair].reshape(slots * pair, nope)
            rows_in = rows_in.astype(BF16)
            h = 16 // drafts * block + 2 * half
            one = jnp.dot(rows_in, keys_ref[h], preferred_element_type=F32)
            two = jnp.dot(rows_in, keys_ref[h + 1], preferred_element_type=F32)
            done.append(jnp.where(first, one, two).reshape(slots, pair, latent))
        query_ref[:, 16 * block : 16 * block + 16, :latent] = jnp.concatenate(done, 1).astype(BF16)
    arrival(blocks).wait()
    half_rows = rows // 2
    query_ref[:, :half_rows, latent:] = arrived_ref[:, rows : rows + half_rows, :rope]
    query_ref[:, half_rows:, latent:] = arrived_ref[:, rows : rows + half_rows, rope : 2 * rope]

    eye = lax.broadcasted_iota(jnp.int32, (rows, vhead), 0) == lax.broadcasted_iota(
        jnp.int32, (rows, vhead), 1
    )
    line = lax.broadcasted_iota(jnp.int32, (16, vhead), 0)
    token = lax.broadcasted_iota(jnp.int32, (rows, tokens), 1)

    for t in range(trips):
        pool_part(t).wait()
        ns = [t * group + k for k in range(group)]
        scores = [
            lax.dot_general(
                query_ref[n], pool_ref[n], (((1,), (1,)), ((), ())), preferred_element_type=F32
            )
            * scale
            for n in ns
        ]
        scores = [jnp.where(token < live_ref[n], x, NEG_FILL) for n, x in zip(ns, scores)]
        tops = [jnp.max(x, axis=1, keepdims=True) for x in scores]
        weights = [jnp.exp(x - top) for x, top in zip(scores, tops)]
        totals = [jnp.sum(x, axis=1, keepdims=True) for x in weights]
        weighted = [
            jnp.dot(x.astype(BF16), pool_ref[n, :, :latent], preferred_element_type=F32)
            for n, x in zip(ns, weights)
        ]
        for n, top, total, x in zip(ns, tops, totals, weighted):
            mean_ref[n] = (x * (1.0 / total)).astype(BF16)
            mass = jnp.sum(jnp.where(eye, top + jnp.log(total), 0.0), axis=0, keepdims=True)
            high = mass.astype(BF16).astype(F32)
            middle = (mass - high).astype(BF16).astype(F32)
            low = mass - high - middle
            parts = jnp.where(line == 0, high, jnp.where(line == 1, middle, low))
            out_ref[n, rows:, :] = jnp.where(line < PARTS, parts, 0.0).astype(BF16)

    leaving(blocks).start()
    values_copy.wait()
    for block in range(blocks):
        part = mean_ref[:, 16 * block : 16 * block + 16, :].astype(F32)
        done = []
        for half in range(16 // pair):
            rows_in = part[:, pair * half : pair * half + pair].reshape(slots * pair, latent)
            rows_in = rows_in.astype(BF16)
            h = 16 // drafts * block + 2 * half
            both = jnp.concatenate([values_ref[h], values_ref[h + 1]], 1)
            both = jnp.dot(rows_in, both, preferred_element_type=F32)
            both = jnp.where(first, both[:, :vhead], both[:, vhead:])
            done.append(both.reshape(slots, pair, vhead))
        out_ref[:, 16 * block : 16 * block + 16, :] = jnp.concatenate(done, 1).astype(BF16)
        leaving(block).start()
    for block in range(blocks + 1):
        leaving(block).wait()


def lend(live, arrived, key_absorb, value_absorb, pool, scale, group=8):
    slots, _, width = pool.shape
    latent = key_absorb.shape[2]
    vhead = value_absorb.shape[-1]
    rows = arrived.shape[1] * 2 // 3
    vmem = pl.BlockSpec(memory_space=pltpu.VMEM)
    hbm = pl.BlockSpec(memory_space=pl.ANY)
    return pl.pallas_call(
        functools.partial(lend_kernel, scale, group),
        out_shape=pltpu.HBM((slots, rows + 16, vhead), BF16),
        in_specs=[pl.BlockSpec(memory_space=pltpu.SMEM), hbm, vmem, hbm, hbm],
        out_specs=pl.BlockSpec(memory_space=pltpu.HBM),
        scratch_shapes=[
            pltpu.VMEM((slots, rows + 16, vhead), BF16),
            pltpu.VMEM(arrived.shape, BF16),
            pltpu.VMEM(value_absorb.shape, BF16),
            pltpu.VMEM(pool.shape, BF16),
            pltpu.VMEM((slots, rows, width), BF16),
            pltpu.VMEM((slots, rows, latent), BF16),
            pltpu.SemaphoreType.DMA((2 * (rows // 16) + 3 + slots // group,)),
        ],
        compiler_params=pltpu.CompilerParams(vmem_limit_bytes=28 * 2**20),
        name="lend",
    )(
        live,
        pltpu.with_memory_space_constraint(arrived, pltpu.HBM),
        key_absorb,
        pltpu.with_memory_space_constraint(value_absorb, pltpu.HBM),
        pltpu.with_memory_space_constraint(pool, pltpu.HBM),
    )


def settle_kernel(back_ref, local_ref, draft_scores_ref, draft_values_ref, out_ref, rows_ref, wide_ref):
    slots, _, vhead = back_ref.shape
    reqs, rows, drafts = draft_scores_ref.shape
    heads = rows // drafts
    mass = jnp.sum(back_ref[:, rows:, :].astype(F32), axis=1)
    mass = jnp.transpose(mass)[:rows]
    local = local_ref[...]
    for i in range(reqs):
        member = local == i
        draft = draft_scores_ref[i]
        own = jnp.where(member, mass, NEG_FILL)
        top = jnp.maximum(
            jnp.max(own, axis=1, keepdims=True), jnp.max(draft, axis=1, keepdims=True)
        )
        weight = jnp.where(member, jnp.exp(own - top), 0.0)
        draft = jnp.exp(draft - top)
        total = jnp.sum(weight, axis=1, keepdims=True) + jnp.sum(draft, axis=1, keepdims=True)
        value = jnp.zeros((rows, vhead), F32)
        for n in range(slots):
            value = value + weight[:, n : n + 1] * back_ref[n, :rows, :].astype(F32)
        for j in range(drafts):
            for s in range(drafts):
                wide_ref[pl.ds(j * rows + s, heads, stride=drafts), :] = draft_values_ref[i, j]
            value = value + draft[:, j : j + 1] * wide_ref[j * rows : (j + 1) * rows]
        value = value / total
        for h in range(heads):
            at = (h * reqs + i) * drafts
            rows_ref[at : at + drafts, :] = value[h * drafts : (h + 1) * drafts]
    size = reqs * drafts
    joined = jnp.concatenate([rows_ref[h * size : (h + 1) * size] for h in range(heads)], 1)
    joined = joined.astype(BF16)
    for n in range(out_ref.shape[0]):
        out_ref[n] = joined


def settle(back, local, draft_scores, draft_values, copies):
    _, _, vhead = back.shape
    reqs, rows, drafts = draft_scores.shape
    vmem = pl.BlockSpec(memory_space=pltpu.VMEM)
    return pl.pallas_call(
        settle_kernel,
        out_shape=jax.ShapeDtypeStruct((copies, reqs * drafts, rows // drafts * vhead), BF16),
        in_specs=[vmem] * 4,
        out_specs=vmem,
        scratch_shapes=[
            pltpu.VMEM((reqs * rows, vhead), F32),
            pltpu.VMEM((drafts * rows, vhead), F32),
        ],
        compiler_params=pltpu.CompilerParams(vmem_limit_bytes=8 * 2**20),
        name="settle",
    )(back, local, draft_scores, draft_values)


def body(
    draft_queries,
    draft_latents,
    latent_pool,
    key_absorb,
    value_absorb,
    out_proj,
    slot_request,
    context_lengths,
):
    home = lax.axis_index("lender")
    reqs, drafts, heads, width = draft_queries.shape
    nope, latent = key_absorb.shape[1:]
    tokens = latent_pool.shape[1]
    rows = heads * drafts
    scale = width ** (-0.5) * MSCALE_SQ

    outgoing = pack(jnp.full((1,), home, jnp.int32), slot_request, draft_queries, nope)
    outgoing, slot_request, context_lengths, draft_queries, draft_latents = (
        lax.optimization_barrier(
            (outgoing, slot_request, context_lengths, draft_queries, draft_latents)
        )
    )
    arrived = lax.all_to_all(outgoing, "lender", split_axis=0, concat_axis=0, tiled=True)

    live_all = live_tokens(slot_request, context_lengths, tokens)
    live_here = lax.dynamic_slice_in_dim(live_all, home, 1, 0)[0]
    local = lax.dynamic_slice_in_dim(slot_request, home, 1, 1).reshape(1, -1) - home * reqs
    part = jnp.einsum(
        "ishc,hcl->ihsl", draft_queries[..., :nope], key_absorb, preferred_element_type=F32
    ).astype(BF16)
    own = jnp.concatenate([part, jnp.swapaxes(draft_queries[..., nope:], 1, 2)], -1)
    draft_scores = (
        jnp.einsum("ihsk,ijk->ihsj", own, draft_latents, preferred_element_type=F32) * scale
    )
    causal = jnp.arange(drafts)[:, None] >= jnp.arange(drafts)[None, :]
    draft_scores = jnp.where(causal, draft_scores, NEG_FILL).reshape(reqs, rows, drafts)
    draft_values = jnp.einsum(
        "ijl,hlc->ijhc", draft_latents[:, :, :latent], value_absorb, preferred_element_type=F32
    )
    arrived, live_here, local, draft_scores, draft_values = lax.optimization_barrier(
        (arrived, live_here, local, draft_scores, draft_values)
    )

    sending = lend(live_here, arrived, key_absorb, value_absorb, latent_pool, scale)
    back = lax.all_to_all(sending, "lender", split_axis=0, concat_axis=0, tiled=True)

    copies = settle(back, local, draft_scores, draft_values, 8)
    lenders = latent_pool.shape[0]
    inner = [[8 * y + z for z in range(8)] for y in range(lenders // 8)]
    outer = [[8 * y + z for y in range(lenders // 8)] for z in range(8)]
    plane = lax.all_to_all(
        copies, "lender", split_axis=0, concat_axis=0, tiled=True, axis_index_groups=inner
    )
    plane = jnp.broadcast_to(plane[None], (lenders // 8,) + plane.shape)
    everyone = lax.all_to_all(
        plane, "lender", split_axis=0, concat_axis=0, tiled=True, axis_index_groups=outer
    )
    partial = jnp.dot(
        everyone.reshape(-1, everyone.shape[-1]), out_proj, preferred_element_type=F32
    ).astype(BF16)
    parts = lax.axis_size("tensor")
    terms = lax.all_to_all(
        partial.reshape(parts, -1, partial.shape[-1]), "tensor", split_axis=0, concat_axis=0
    )
    mixed = jnp.sum(terms.astype(F32), axis=0).astype(BF16)
    return mixed.reshape(-1, drafts, partial.shape[-1])


def solution(mesh):
    in_specs = (
        P("lender", None, "tensor", None),
        P("lender", None, None),
        P("lender", None, None),
        P("tensor", None, None),
        P("tensor", None, None),
        P("tensor", "lender"),
        P(),
        P(),
    )
    out_specs = P("tensor", None, "lender")
    return jax.shard_map(body, mesh=mesh, in_specs=in_specs, out_specs=out_specs, check_vma=False)
```

```python
import functools
import math

import jax
import jax.numpy as jnp
from jax import lax
from jax.experimental import pallas as pl
from jax.experimental.pallas import tpu as pltpu
from jax.sharding import PartitionSpec as P

MSCALE_SQ = (0.1 * math.log(40.0) + 1.0) ** 2
NEG_FILL = -1e30
BF16 = jnp.bfloat16
F32 = jnp.float32
PARTS = 3


def live_tokens(slot_request, context_lengths, slot_tokens):
    lenders = slot_request.shape[0]
    owners = jnp.arange(context_lengths.shape[0], dtype=jnp.int32)
    lengths = jnp.sum(
        jnp.where(
            slot_request[:, :, None] == owners[None, None, :], context_lengths[None, None, :], 0
        ),
        axis=-1,
    )
    matching = slot_request[:, None, :] == slot_request[None, :, :]
    before = jnp.arange(lenders)[:, None] < jnp.arange(lenders)[None, :]
    slot_rank = jnp.sum(jnp.where(matching & before[:, :, None], 1, 0), axis=0)
    return jnp.clip(lengths - slot_tokens * slot_rank, 0, slot_tokens)


def pack_kernel(
    home_ref, slot_request_ref, queries_ref, out_ref, nope_ref, rope_ref, packed_ref, sems
):
    reqs, drafts, heads, width = queries_ref.shape
    nope = nope_ref.shape[-1]
    half = heads * drafts // 2
    for i in range(reqs):
        for s in range(drafts):
            x = queries_ref[i, s].astype(F32)
            nope_ref[pl.ds(s, heads, stride=drafts), :] = x[:, :nope]
            rope_ref[pl.ds(s, heads, stride=drafts), :] = x[:, nope:]
        rope = rope_ref[...]
        rope = jnp.concatenate([rope[:half], rope[half:]], 1)
        packed_ref[i] = jnp.concatenate([nope_ref[...], rope], 0).astype(BF16)
    home = home_ref[0]
    copies = [
        pltpu.make_async_copy(
            packed_ref.at[jnp.clip(slot_request_ref[d, home] - home * reqs, 0, reqs - 1)],
            out_ref.at[d],
            sems.at[d],
        )
        for d in range(out_ref.shape[0])
    ]
    for copy in copies:
        copy.start()
    for copy in copies:
        copy.wait()


def pack(home, slot_request, queries, nope):
    reqs, drafts, heads, width = queries.shape
    rows = heads * drafts
    smem = pl.BlockSpec(memory_space=pltpu.SMEM)
    vmem = pl.BlockSpec(memory_space=pltpu.VMEM)
    slots = slot_request.shape[0]
    return pl.pallas_call(
        pack_kernel,
        out_shape=pltpu.HBM((slots, rows + rows // 2, nope), BF16),
        in_specs=[smem, smem, vmem],
        out_specs=pl.BlockSpec(memory_space=pltpu.HBM),
        scratch_shapes=[
            pltpu.VMEM((rows, nope), F32),
            pltpu.VMEM((rows, width - nope), F32),
            pltpu.VMEM((reqs, rows + rows // 2, nope), BF16),
            pltpu.SemaphoreType.DMA((slots,)),
        ],
        name="pack",
    )(home, slot_request, queries)


def lend_kernel(
    scale,
    group,
    live_ref,
    arrived_any,
    keys_ref,
    values_any,
    pool_any,
    out_any,
    out_ref,
    arrived_ref,
    values_ref,
    pool_ref,
    query_ref,
    mean_ref,
    sems,
):
    slots, _, nope = arrived_ref.shape
    heads, _, latent = keys_ref.shape
    vhead = values_ref.shape[-1]
    rows, width = query_ref.shape[1:]
    drafts = rows // heads
    rope = width - latent
    tokens = pool_ref.shape[1]
    pair = 2 * drafts
    blocks = rows // 16
    trips = slots // group

    def arrival(b):
        at = pl.ds(16 * b, 16) if b < blocks else pl.ds(rows, rows // 2)
        return pltpu.make_async_copy(arrived_any.at[:, at], arrived_ref.at[:, at], sems.at[b])

    def pool_part(t):
        at = pl.ds(t * group, group)
        return pltpu.make_async_copy(pool_any.at[at], pool_ref.at[at], sems.at[blocks + 2 + t])

    def leaving(t):
        at = pl.ds(t * group, group)
        return pltpu.make_async_copy(out_ref.at[at], out_any.at[at], sems.at[blocks + 2 + trips + t])

    def project(at, count):
        for block in range(blocks):
            part = mean_ref[at : at + count, 16 * block : 16 * block + 16, :].astype(F32)
            done = []
            for half in range(16 // pair):
                rows_in = part[:, pair * half : pair * half + pair].reshape(count * pair, latent)
                h = 16 // drafts * block + 2 * half
                both = jnp.concatenate([values_ref[h], values_ref[h + 1]], 1)
                both = jnp.dot(rows_in.astype(BF16), both, preferred_element_type=F32)
                both = jnp.where(first[: count * pair], both[:, :vhead], both[:, vhead:])
                done.append(both.reshape(count, pair, vhead))
            done = jnp.concatenate(done, 1).astype(BF16)
            out_ref[at : at + count, 16 * block : 16 * block + 16, :] = done

    values_copy = pltpu.make_async_copy(values_any, values_ref, sems.at[blocks + 1])
    for b in range(blocks + 1):
        arrival(b).start()
    for t in range(trips):
        pool_part(t).start()
    values_copy.start()

    first = lax.broadcasted_iota(jnp.int32, (slots * pair, 1), 0) % pair < drafts

    for block in range(blocks):
        arrival(block).wait()
        part = arrived_ref[:, 16 * block : 16 * block + 16, :].astype(F32)
        done = []
        for half in range(16 // pair):
            rows_in = part[:, pair * half : pair * half + pair].reshape(slots * pair, nope)
            rows_in = rows_in.astype(BF16)
            h = 16 // drafts * block + 2 * half
            one = jnp.dot(rows_in, keys_ref[h], preferred_element_type=F32)
            two = jnp.dot(rows_in, keys_ref[h + 1], preferred_element_type=F32)
            done.append(jnp.where(first, one, two).reshape(slots, pair, latent))
        query_ref[:, 16 * block : 16 * block + 16, :latent] = jnp.concatenate(done, 1).astype(BF16)
    arrival(blocks).wait()
    half_rows = rows // 2
    query_ref[:, :half_rows, latent:] = arrived_ref[:, rows : rows + half_rows, :rope]
    query_ref[:, half_rows:, latent:] = arrived_ref[:, rows : rows + half_rows, rope : 2 * rope]

    eye = lax.broadcasted_iota(jnp.int32, (rows, vhead), 0) == lax.broadcasted_iota(
        jnp.int32, (rows, vhead), 1
    )
    line = lax.broadcasted_iota(jnp.int32, (8, vhead), 0)
    token = lax.broadcasted_iota(jnp.int32, (rows, tokens), 1)

    for t in range(trips):
        pool_part(t).wait()
        ns = [t * group + k for k in range(group)]
        scores = [
            lax.dot_general(
                query_ref[n], pool_ref[n], (((1,), (1,)), ((), ())), preferred_element_type=F32
            )
            * scale
            for n in ns
        ]
        scores = [jnp.where(token < live_ref[n], x, NEG_FILL) for n, x in zip(ns, scores)]
        tops = [jnp.max(x, axis=1, keepdims=True) for x in scores]
        weights = [jnp.exp(x - top) for x, top in zip(scores, tops)]
        totals = [jnp.sum(x, axis=1, keepdims=True) for x in weights]
        weighted = [
            jnp.dot(x.astype(BF16), pool_ref[n, :, :latent], preferred_element_type=F32)
            for n, x in zip(ns, weights)
        ]
        for n, top, total, x in zip(ns, tops, totals, weighted):
            mean_ref[n] = (x * (1.0 / total)).astype(BF16)
            mass = jnp.sum(jnp.where(eye, top + jnp.log(total), 0.0), axis=0, keepdims=True)
            high = mass.astype(BF16).astype(F32)
            middle = (mass - high).astype(BF16).astype(F32)
            low = mass - high - middle
            parts = jnp.where(line == 0, high, jnp.where(line == 1, middle, low))
            out_ref[n, rows:, :] = jnp.where(line < PARTS, parts, 0.0).astype(BF16)
        if t % 2 == 1:
            if t == 1:
                values_copy.wait()
            project((t - 1) * group, 2 * group)
            leaving(t - 1).start()
            leaving(t).start()
    for t in range(trips):
        leaving(t).wait()


def lend(live, arrived, key_absorb, value_absorb, pool, scale, group=8):
    slots, _, width = pool.shape
    latent = key_absorb.shape[2]
    vhead = value_absorb.shape[-1]
    rows = arrived.shape[1] * 2 // 3
    vmem = pl.BlockSpec(memory_space=pltpu.VMEM)
    hbm = pl.BlockSpec(memory_space=pl.ANY)
    return pl.pallas_call(
        functools.partial(lend_kernel, scale, group),
        out_shape=pltpu.HBM((slots, rows + 8, vhead), BF16),
        in_specs=[pl.BlockSpec(memory_space=pltpu.SMEM), hbm, vmem, hbm, hbm],
        out_specs=pl.BlockSpec(memory_space=pltpu.HBM),
        scratch_shapes=[
            pltpu.VMEM((slots, rows + 8, vhead), BF16),
            pltpu.VMEM(arrived.shape, BF16),
            pltpu.VMEM(value_absorb.shape, BF16),
            pltpu.VMEM(pool.shape, BF16),
            pltpu.VMEM((slots, rows, width), BF16),
            pltpu.VMEM((slots, rows, latent), BF16),
            pltpu.SemaphoreType.DMA((rows // 16 + 2 + 2 * (slots // group),)),
        ],
        compiler_params=pltpu.CompilerParams(vmem_limit_bytes=28 * 2**20),
        name="lend",
    )(
        live,
        arrived,
        key_absorb,
        pltpu.with_memory_space_constraint(value_absorb, pltpu.HBM),
        pltpu.with_memory_space_constraint(pool, pltpu.HBM),
    )


def settle_kernel(back_ref, local_ref, draft_scores_ref, draft_values_ref, out_ref, rows_ref, wide_ref):
    slots, _, vhead = back_ref.shape
    reqs, rows, drafts = draft_scores_ref.shape
    heads = rows // drafts
    mass = jnp.sum(back_ref[:, rows:, :].astype(F32), axis=1)
    mass = jnp.transpose(mass)[:rows]
    local = local_ref[...]
    for i in range(reqs):
        member = local == i
        draft = draft_scores_ref[i]
        own = jnp.where(member, mass, NEG_FILL)
        top = jnp.maximum(
            jnp.max(own, axis=1, keepdims=True), jnp.max(draft, axis=1, keepdims=True)
        )
        weight = jnp.where(member, jnp.exp(own - top), 0.0)
        draft = jnp.exp(draft - top)
        total = jnp.sum(weight, axis=1, keepdims=True) + jnp.sum(draft, axis=1, keepdims=True)
        value = jnp.zeros((rows, vhead), F32)
        for n in range(slots):
            value = value + weight[:, n : n + 1] * back_ref[n, :rows, :].astype(F32)
        for j in range(drafts):
            for s in range(drafts):
                wide_ref[pl.ds(j * rows + s, heads, stride=drafts), :] = draft_values_ref[i, j]
            value = value + draft[:, j : j + 1] * wide_ref[j * rows : (j + 1) * rows]
        value = value / total
        for h in range(heads):
            at = (h * reqs + i) * drafts
            rows_ref[at : at + drafts, :] = value[h * drafts : (h + 1) * drafts]
    size = reqs * drafts
    joined = jnp.concatenate([rows_ref[h * size : (h + 1) * size] for h in range(heads)], 1)
    joined = joined.astype(BF16)
    for n in range(out_ref.shape[0]):
        out_ref[n] = joined


def settle(back, local, draft_scores, draft_values, copies):
    _, _, vhead = back.shape
    reqs, rows, drafts = draft_scores.shape
    vmem = pl.BlockSpec(memory_space=pltpu.VMEM)
    return pl.pallas_call(
        settle_kernel,
        out_shape=jax.ShapeDtypeStruct((copies, reqs * drafts, rows // drafts * vhead), BF16),
        in_specs=[vmem] * 4,
        out_specs=vmem,
        scratch_shapes=[
            pltpu.VMEM((reqs * rows, vhead), F32),
            pltpu.VMEM((drafts * rows, vhead), F32),
        ],
        compiler_params=pltpu.CompilerParams(vmem_limit_bytes=8 * 2**20),
        name="settle",
    )(back, local, draft_scores, draft_values)


def mix_kernel(place_ref, rows_ref, *refs):
    weights, (own_ref, other_ref, late_ref, held_ref, sem) = list(refs[:-5]), refs[-5:]
    blocks, size = own_ref.shape[:2]
    late = pltpu.make_async_copy(weights[blocks - 1], late_ref, sem)
    late.start()
    weights[blocks - 1] = late_ref
    half = rows_ref.shape[1] // 2
    dot = functools.partial(
        lax.dot_general,
        dimension_numbers=(((1,), (1,)), ((), ())),
        preferred_element_type=F32,
    )
    for k in range(blocks):
        if k == blocks - 1:
            late.wait()
        if k == blocks // 2:
            done = dot(rows_ref[:, :half], weights[k][...])
            done += dot(rows_ref[:, half:], weights[blocks][...])
        else:
            done = dot(rows_ref[...], weights[k][...])
        held_ref[k] = done.astype(BF16)
    core = place_ref[blocks]
    for k in range(blocks):
        first = held_ref[place_ref[k], :size, :]
        second = held_ref[place_ref[k], size:, :]
        own_ref[k] = jnp.where(core == 0, first, second)
        other_ref[k] = jnp.where(core == 0, second, first)


def mix(place, rows, weights):
    blocks = place.shape[0] - 1
    features = weights[0].shape[0]
    vmem = pl.BlockSpec(memory_space=pltpu.VMEM)
    half = jax.ShapeDtypeStruct((blocks, rows.shape[0] // 2, features), BF16)
    return pl.pallas_call(
        mix_kernel,
        out_shape=[half, half],
        in_specs=[
            pl.BlockSpec(memory_space=pltpu.SMEM),
            vmem,
            *[pl.BlockSpec(memory_space=pl.ANY) if i == blocks - 1 else vmem for i in range(5)],
        ],
        out_specs=[vmem, vmem],
        scratch_shapes=[
            pltpu.VMEM(weights[0].shape, BF16),
            pltpu.VMEM((blocks, rows.shape[0], features), BF16),
            pltpu.SemaphoreType.DMA,
        ],
        compiler_params=pltpu.CompilerParams(vmem_limit_bytes=12 * 2**20),
        name="mix",
    )(place, rows, *weights)


def body(
    draft_queries,
    draft_latents,
    latent_pool,
    key_absorb,
    value_absorb,
    out_proj,
    slot_request,
    context_lengths,
):
    home = lax.axis_index("lender")
    reqs, drafts, heads, width = draft_queries.shape
    nope, latent = key_absorb.shape[1:]
    tokens = latent_pool.shape[1]
    rows = heads * drafts
    scale = width ** (-0.5) * MSCALE_SQ

    outgoing = pack(jnp.full((1,), home, jnp.int32), slot_request, draft_queries, nope)
    outgoing, slot_request, context_lengths, draft_queries, draft_latents, out_proj = (
        lax.optimization_barrier(
            (outgoing, slot_request, context_lengths, draft_queries, draft_latents, out_proj)
        )
    )
    arrived = lax.all_to_all(outgoing, "lender", split_axis=0, concat_axis=0, tiled=True)

    live_all = live_tokens(slot_request, context_lengths, tokens)
    live_here = lax.dynamic_slice_in_dim(live_all, home, 1, 0)[0]
    local = lax.dynamic_slice_in_dim(slot_request, home, 1, 1).reshape(1, -1) - home * reqs
    lenders, column = latent_pool.shape[0], 8
    planes = lenders // column
    up = [(l, (l - column) % lenders) for l in range(lenders)]
    down = [(l, (l + column) % lenders) for l in range(lenders)]
    out_proj, local = lax.optimization_barrier((out_proj, local))
    weight = out_proj.T
    half = weight.shape[1] // 2
    weight_up = lax.ppermute(weight, "lender", up)
    weight_down = lax.ppermute(weight, "lender", down)

    part = jnp.einsum(
        "ishc,hcl->ihsl", draft_queries[..., :nope], key_absorb, preferred_element_type=F32
    ).astype(BF16)
    own = jnp.concatenate([part, jnp.swapaxes(draft_queries[..., nope:], 1, 2)], -1)
    draft_scores = (
        jnp.einsum("ihsk,ijk->ihsj", own, draft_latents, preferred_element_type=F32) * scale
    )
    causal = jnp.arange(drafts)[:, None] >= jnp.arange(drafts)[None, :]
    draft_scores = jnp.where(causal, draft_scores, NEG_FILL).reshape(reqs, rows, drafts)
    draft_values = jnp.einsum(
        "ijl,hlc->ijhc", draft_latents[:, :, :latent], value_absorb, preferred_element_type=F32
    )
    arrived, live_here, local, draft_scores, draft_values = lax.optimization_barrier(
        (arrived, live_here, local, draft_scores, draft_values)
    )

    sending = lend(live_here, arrived, key_absorb, value_absorb, latent_pool, scale)
    sending, weight_up, weight_down = lax.optimization_barrier((sending, weight_up, weight_down))
    back = lax.all_to_all(sending, "lender", split_axis=0, concat_axis=0, tiled=True)
    far_left = lax.ppermute(weight_up[:, :half], "lender", up)
    far_right = lax.ppermute(weight_down[:, half:], "lender", down)

    copies = settle(back, local, draft_scores, draft_values, column)
    inner = [[column * y + z for z in range(column)] for y in range(planes)]
    plane = lax.all_to_all(
        copies, "lender", split_axis=0, concat_axis=0, tiled=True, axis_index_groups=inner
    )
    plane, far_left, far_right = lax.optimization_barrier((plane, far_left, far_right))
    y = home // column
    tensor = lax.axis_index("tensor")
    x, core = tensor // 2, tensor % 2
    place = jnp.stack([(k - y) % planes for k in range(planes)] + [core]).astype(jnp.int32)
    weight_down = pltpu.with_memory_space_constraint(weight_down, pltpu.HBM)
    weights = [weight, weight_up, far_left, weight_down, far_right]
    own, other = mix(place, plane.reshape(-1, plane.shape[-1]), weights)

    tensors = lax.axis_size("tensor")
    swap = [(t, t ^ 1) for t in range(tensors)]
    own = (own.astype(F32) + lax.ppermute(other, "tensor", swap).astype(F32)).astype(BF16)
    chunks = jnp.broadcast_to(own[:, None], (planes, tensors // 2) + own.shape[1:])
    chunks = chunks.reshape((planes * tensors // 2,) + own.shape[1:])
    groups = [
        [(column * p + z) * tensors + 2 * q + c for p in range(planes) for q in range(tensors // 2)]
        for z in range(column)
        for c in range(2)
    ]
    terms = lax.all_to_all(
        chunks,
        ("lender", "tensor"),
        split_axis=0,
        concat_axis=0,
        tiled=True,
        axis_index_groups=groups,
    )
    terms = lax.dynamic_slice_in_dim(terms, x * (tensors // 2), tensors // 2, 0)
    total = jnp.sum(terms.astype(F32), axis=0)
    return total.astype(BF16).reshape(-1, drafts, total.shape[-1])


def solution(mesh):
    in_specs = (
        P("lender", None, "tensor", None),
        P("lender", None, None),
        P("lender", None, None),
        P("tensor", None, None),
        P("tensor", None, None),
        P("tensor", "lender"),
        P(),
        P(),
    )
    out_specs = P("tensor", None, "lender")
    return jax.shard_map(body, mesh=mesh, in_specs=in_specs, out_specs=out_specs, check_vma=False)
```

```python
import functools
import math

import jax
import jax.numpy as jnp
from jax import lax
from jax.experimental import pallas as pl
from jax.experimental.pallas import tpu as pltpu
from jax.sharding import PartitionSpec as P

MSCALE_SQ = (0.1 * math.log(40.0) + 1.0) ** 2
NEG_FILL = -1e30
BF16 = jnp.bfloat16
F32 = jnp.float32
PARTS = 3


def live_tokens(slot_request, context_lengths, slot_tokens):
    lenders = slot_request.shape[0]
    owners = jnp.arange(context_lengths.shape[0], dtype=jnp.int32)
    lengths = jnp.sum(
        jnp.where(
            slot_request[:, :, None] == owners[None, None, :], context_lengths[None, None, :], 0
        ),
        axis=-1,
    )
    matching = slot_request[:, None, :] == slot_request[None, :, :]
    before = jnp.arange(lenders)[:, None] < jnp.arange(lenders)[None, :]
    slot_rank = jnp.sum(jnp.where(matching & before[:, :, None], 1, 0), axis=0)
    return jnp.clip(lengths - slot_tokens * slot_rank, 0, slot_tokens)


def pack_kernel(
    home_ref, slot_request_ref, queries_ref, out_ref, nope_ref, rope_ref, packed_ref, sems
):
    reqs, drafts, heads, width = queries_ref.shape
    nope = nope_ref.shape[-1]
    half = heads * drafts // 2
    for i in range(reqs):
        for s in range(drafts):
            x = queries_ref[i, s].astype(F32)
            nope_ref[pl.ds(s, heads, stride=drafts), :] = x[:, :nope]
            rope_ref[pl.ds(s, heads, stride=drafts), :] = x[:, nope:]
        rope = rope_ref[...]
        rope = jnp.concatenate([rope[:half], rope[half:]], 1)
        packed_ref[i] = jnp.concatenate([nope_ref[...], rope], 0).astype(BF16)
    home = home_ref[0]
    copies = [
        pltpu.make_async_copy(
            packed_ref.at[jnp.clip(slot_request_ref[d, home] - home * reqs, 0, reqs - 1)],
            out_ref.at[d],
            sems.at[d],
        )
        for d in range(out_ref.shape[0])
    ]
    for copy in copies:
        copy.start()
    for copy in copies:
        copy.wait()


def pack(home, slot_request, queries, nope):
    reqs, drafts, heads, width = queries.shape
    rows = heads * drafts
    smem = pl.BlockSpec(memory_space=pltpu.SMEM)
    vmem = pl.BlockSpec(memory_space=pltpu.VMEM)
    slots = slot_request.shape[0]
    return pl.pallas_call(
        pack_kernel,
        out_shape=pltpu.HBM((slots, rows + rows // 2, nope), BF16),
        in_specs=[smem, smem, vmem],
        out_specs=pl.BlockSpec(memory_space=pltpu.HBM),
        scratch_shapes=[
            pltpu.VMEM((rows, nope), F32),
            pltpu.VMEM((rows, width - nope), F32),
            pltpu.VMEM((reqs, rows + rows // 2, nope), BF16),
            pltpu.SemaphoreType.DMA((slots,)),
        ],
        name="pack",
    )(home, slot_request, queries)


def lend_kernel(
    scale,
    group,
    live_ref,
    arrived_ref,
    keys_ref,
    values_any,
    pool_any,
    out_any,
    out_ref,
    values_ref,
    pool_ref,
    query_ref,
    mean_ref,
    sems,
):
    slots, _, nope = arrived_ref.shape
    heads, _, latent = keys_ref.shape
    vhead = values_ref.shape[-1]
    rows, width = query_ref.shape[1:]
    drafts = rows // heads
    rope = width - latent
    tokens = pool_ref.shape[1]
    pair = 2 * drafts
    blocks = rows // 16
    trips = slots // group

    def pool_part(t):
        at = pl.ds(t * group, group)
        return pltpu.make_async_copy(pool_any.at[at], pool_ref.at[at], sems.at[t])

    def leaving(t):
        at = pl.ds(t * group, group)
        return pltpu.make_async_copy(out_ref.at[at], out_any.at[at], sems.at[trips + t])

    def project(at, count):
        for block in range(blocks):
            part = mean_ref[at : at + count, 16 * block : 16 * block + 16, :].astype(F32)
            done = []
            for half in range(16 // pair):
                rows_in = part[:, pair * half : pair * half + pair].reshape(count * pair, latent)
                h = 16 // drafts * block + 2 * half
                both = jnp.concatenate([values_ref[h], values_ref[h + 1]], 1)
                both = jnp.dot(rows_in.astype(BF16), both, preferred_element_type=F32)
                both = jnp.where(first[: count * pair], both[:, :vhead], both[:, vhead:])
                done.append(both.reshape(count, pair, vhead))
            done = jnp.concatenate(done, 1).astype(BF16)
            out_ref[at : at + count, 16 * block : 16 * block + 16, :] = done

    values_copy = pltpu.make_async_copy(values_any, values_ref, sems.at[2 * trips])
    for t in range(trips):
        pool_part(t).start()
    values_copy.start()

    first = lax.broadcasted_iota(jnp.int32, (slots * pair, 1), 0) % pair < drafts

    for block in range(blocks):
        part = arrived_ref[:, 16 * block : 16 * block + 16, :].astype(F32)
        done = []
        for half in range(16 // pair):
            rows_in = part[:, pair * half : pair * half + pair].reshape(slots * pair, nope)
            rows_in = rows_in.astype(BF16)
            h = 16 // drafts * block + 2 * half
            one = jnp.dot(rows_in, keys_ref[h], preferred_element_type=F32)
            two = jnp.dot(rows_in, keys_ref[h + 1], preferred_element_type=F32)
            done.append(jnp.where(first, one, two).reshape(slots, pair, latent))
        query_ref[:, 16 * block : 16 * block + 16, :latent] = jnp.concatenate(done, 1).astype(BF16)
    half_rows = rows // 2
    query_ref[:, :half_rows, latent:] = arrived_ref[:, rows : rows + half_rows, :rope]
    query_ref[:, half_rows:, latent:] = arrived_ref[:, rows : rows + half_rows, rope : 2 * rope]

    eye = lax.broadcasted_iota(jnp.int32, (rows, vhead), 0) == lax.broadcasted_iota(
        jnp.int32, (rows, vhead), 1
    )
    line = lax.broadcasted_iota(jnp.int32, (8, vhead), 0)
    token = lax.broadcasted_iota(jnp.int32, (rows, tokens), 1)

    for t in range(trips):
        pool_part(t).wait()
        ns = [t * group + k for k in range(group)]
        scores = [
            lax.dot_general(
                query_ref[n], pool_ref[n], (((1,), (1,)), ((), ())), preferred_element_type=F32
            )
            * scale
            for n in ns
        ]
        scores = [jnp.where(token < live_ref[n], x, NEG_FILL) for n, x in zip(ns, scores)]
        tops = [jnp.max(x, axis=1, keepdims=True) for x in scores]
        weights = [jnp.exp(x - top) for x, top in zip(scores, tops)]
        totals = [jnp.sum(x, axis=1, keepdims=True) for x in weights]
        weighted = [
            jnp.dot(x.astype(BF16), pool_ref[n, :, :latent], preferred_element_type=F32)
            for n, x in zip(ns, weights)
        ]
        for n, top, total, x in zip(ns, tops, totals, weighted):
            mean_ref[n] = (x * (1.0 / total)).astype(BF16)
            mass = jnp.sum(jnp.where(eye, top + jnp.log(total), 0.0), axis=0, keepdims=True)
            high = mass.astype(BF16).astype(F32)
            middle = (mass - high).astype(BF16).astype(F32)
            low = mass - high - middle
            parts = jnp.where(line == 0, high, jnp.where(line == 1, middle, low))
            out_ref[n, rows:, :] = jnp.where(line < PARTS, parts, 0.0).astype(BF16)
        if t % 2 == 1:
            if t == 1:
                values_copy.wait()
            project((t - 1) * group, 2 * group)
            leaving(t - 1).start()
            leaving(t).start()
    for t in range(trips):
        leaving(t).wait()


def lend(live, arrived, key_absorb, value_absorb, pool, scale, group=8):
    slots, _, width = pool.shape
    latent = key_absorb.shape[2]
    vhead = value_absorb.shape[-1]
    rows = arrived.shape[1] * 2 // 3
    vmem = pl.BlockSpec(memory_space=pltpu.VMEM)
    hbm = pl.BlockSpec(memory_space=pl.ANY)
    return pl.pallas_call(
        functools.partial(lend_kernel, scale, group),
        out_shape=pltpu.HBM((slots, rows + 8, vhead), BF16),
        in_specs=[pl.BlockSpec(memory_space=pltpu.SMEM), vmem, vmem, hbm, hbm],
        out_specs=pl.BlockSpec(memory_space=pltpu.HBM),
        scratch_shapes=[
            pltpu.VMEM((slots, rows + 8, vhead), BF16),
            pltpu.VMEM(value_absorb.shape, BF16),
            pltpu.VMEM(pool.shape, BF16),
            pltpu.VMEM((slots, rows, width), BF16),
            pltpu.VMEM((slots, rows, latent), BF16),
            pltpu.SemaphoreType.DMA((2 * (slots // group) + 1,)),
        ],
        compiler_params=pltpu.CompilerParams(vmem_limit_bytes=28 * 2**20),
        name="lend",
    )(
        live,
        arrived,
        key_absorb,
        pltpu.with_memory_space_constraint(value_absorb, pltpu.HBM),
        pltpu.with_memory_space_constraint(pool, pltpu.HBM),
    )


def settle_kernel(back_ref, local_ref, draft_scores_ref, draft_values_ref, out_ref, rows_ref, wide_ref):
    slots, _, vhead = back_ref.shape
    reqs, rows, drafts = draft_scores_ref.shape
    heads = rows // drafts
    mass = jnp.sum(back_ref[:, rows:, :].astype(F32), axis=1)
    mass = jnp.transpose(mass)[:rows]
    local = local_ref[...]
    for i in range(reqs):
        member = local == i
        draft = draft_scores_ref[i]
        own = jnp.where(member, mass, NEG_FILL)
        top = jnp.maximum(
            jnp.max(own, axis=1, keepdims=True), jnp.max(draft, axis=1, keepdims=True)
        )
        weight = jnp.where(member, jnp.exp(own - top), 0.0)
        draft = jnp.exp(draft - top)
        total = jnp.sum(weight, axis=1, keepdims=True) + jnp.sum(draft, axis=1, keepdims=True)
        value = jnp.zeros((rows, vhead), F32)
        for n in range(slots):
            value = value + weight[:, n : n + 1] * back_ref[n, :rows, :].astype(F32)
        for j in range(drafts):
            for s in range(drafts):
                wide_ref[pl.ds(j * rows + s, heads, stride=drafts), :] = draft_values_ref[i, j]
            value = value + draft[:, j : j + 1] * wide_ref[j * rows : (j + 1) * rows]
        value = value / total
        for h in range(heads):
            at = (h * reqs + i) * drafts
            rows_ref[at : at + drafts, :] = value[h * drafts : (h + 1) * drafts]
    size = reqs * drafts
    joined = jnp.concatenate([rows_ref[h * size : (h + 1) * size] for h in range(heads)], 1)
    joined = joined.astype(BF16)
    for n in range(out_ref.shape[0]):
        out_ref[n] = joined


def settle(back, local, draft_scores, draft_values, copies):
    _, _, vhead = back.shape
    reqs, rows, drafts = draft_scores.shape
    vmem = pl.BlockSpec(memory_space=pltpu.VMEM)
    return pl.pallas_call(
        settle_kernel,
        out_shape=jax.ShapeDtypeStruct((copies, reqs * drafts, rows // drafts * vhead), BF16),
        in_specs=[vmem] * 4,
        out_specs=vmem,
        scratch_shapes=[
            pltpu.VMEM((reqs * rows, vhead), F32),
            pltpu.VMEM((drafts * rows, vhead), F32),
        ],
        compiler_params=pltpu.CompilerParams(vmem_limit_bytes=8 * 2**20),
        name="settle",
    )(back, local, draft_scores, draft_values)


def mix_kernel(place_ref, rows_ref, *refs):
    weights, (own_ref, other_ref, late_ref, held_ref, sems) = refs[:-5], refs[-5:]
    blocks = own_ref.shape[0]
    size, features = held_ref.shape[-2] // 2, held_ref.shape[-1]
    late = {
        k: pltpu.make_async_copy(weights[k], late_ref.at[n], sems.at[n])
        for n, k in enumerate((1, 2))
    }
    for copy in late.values():
        copy.start()
    dot = functools.partial(
        lax.dot_general,
        dimension_numbers=(((1,), (1,)), ((), ())),
        preferred_element_type=F32,
    )
    for k in (0, 3, 1, 2):
        if k in late:
            late[k].wait()
        done = dot(rows_ref[...], late_ref[k - 1] if k in late else weights[k][...])
        held_ref[k] = done
    core = place_ref[blocks]
    for k in range(blocks):
        both = [held_ref[place_ref[k], n * size : (n + 1) * size, :] for n in range(2)]
        for n, out_ref in enumerate((own_ref, other_ref)):
            piece = jnp.where(core == n, both[0], both[1])
            out_ref[k] = piece.reshape(own_ref.shape[1:]).astype(BF16)


def mix(place, rows, weights, drafts):
    blocks = place.shape[0] - 1
    features = weights[0].shape[0]
    vmem = pl.BlockSpec(memory_space=pltpu.VMEM)
    half = jax.ShapeDtypeStruct((blocks, rows.shape[0] // 2 // drafts, drafts, features), BF16)
    return pl.pallas_call(
        mix_kernel,
        out_shape=[half, half],
        in_specs=[
            pl.BlockSpec(memory_space=pltpu.SMEM),
            vmem,
            *[pl.BlockSpec(memory_space=pl.ANY) if i in (1, 2) else vmem for i in range(blocks)],
        ],
        out_specs=[vmem, vmem],
        scratch_shapes=[
            pltpu.VMEM((2,) + weights[0].shape, BF16),
            pltpu.VMEM((blocks, rows.shape[0], features), F32),
            pltpu.SemaphoreType.DMA((2,)),
        ],
        compiler_params=pltpu.CompilerParams(vmem_limit_bytes=12 * 2**20),
        name="mix",
    )(place, rows, *weights)


def body(
    draft_queries,
    draft_latents,
    latent_pool,
    key_absorb,
    value_absorb,
    out_proj,
    slot_request,
    context_lengths,
):
    home = lax.axis_index("lender")
    reqs, drafts, heads, width = draft_queries.shape
    nope, latent = key_absorb.shape[1:]
    tokens = latent_pool.shape[1]
    rows = heads * drafts
    scale = width ** (-0.5) * MSCALE_SQ

    outgoing = pack(jnp.full((1,), home, jnp.int32), slot_request, draft_queries, nope)
    outgoing, slot_request, context_lengths, draft_queries, draft_latents, out_proj = (
        lax.optimization_barrier(
            (outgoing, slot_request, context_lengths, draft_queries, draft_latents, out_proj)
        )
    )
    arrived = lax.all_to_all(outgoing, "lender", split_axis=0, concat_axis=0, tiled=True)

    live_all = live_tokens(slot_request, context_lengths, tokens)
    live_here = lax.dynamic_slice_in_dim(live_all, home, 1, 0)[0]
    local = lax.dynamic_slice_in_dim(slot_request, home, 1, 1).reshape(1, -1) - home * reqs
    lenders, column = latent_pool.shape[0], 8
    planes = lenders // column
    up = [(l, (l - column) % lenders) for l in range(lenders)]
    down = [(l, (l + column) % lenders) for l in range(lenders)]
    weight = out_proj.T
    weight_up = lax.ppermute(weight, "lender", up)

    part = jnp.einsum(
        "ishc,hcl->ihsl", draft_queries[..., :nope], key_absorb, preferred_element_type=F32
    ).astype(BF16)
    own = jnp.concatenate([part, jnp.swapaxes(draft_queries[..., nope:], 1, 2)], -1)
    draft_scores = (
        jnp.einsum("ihsk,ijk->ihsj", own, draft_latents, preferred_element_type=F32) * scale
    )
    causal = jnp.arange(drafts)[:, None] >= jnp.arange(drafts)[None, :]
    draft_scores = jnp.where(causal, draft_scores, NEG_FILL).reshape(reqs, rows, drafts)
    draft_values = jnp.einsum(
        "ijl,hlc->ijhc", draft_latents[:, :, :latent], value_absorb, preferred_element_type=F32
    )
    arrived, live_here, local, draft_scores, draft_values = lax.optimization_barrier(
        (arrived, live_here, local, draft_scores, draft_values)
    )

    sending = lend(live_here, arrived, key_absorb, value_absorb, latent_pool, scale)
    sending, weight = lax.optimization_barrier((sending, weight))
    back = lax.all_to_all(sending, "lender", split_axis=0, concat_axis=0, tiled=True)
    weight_far = lax.ppermute(weight_up, "lender", up)
    weight_down = lax.ppermute(weight, "lender", down)

    copies = settle(back, local, draft_scores, draft_values, column)
    inner = [[column * y + z for z in range(column)] for y in range(planes)]
    plane = lax.all_to_all(
        copies, "lender", split_axis=0, concat_axis=0, tiled=True, axis_index_groups=inner
    )
    plane, weight_far, weight_down = lax.optimization_barrier((plane, weight_far, weight_down))
    y = home // column
    tensor = lax.axis_index("tensor")
    x, core = tensor // 2, tensor % 2
    place = jnp.stack([(x + k - y) % planes for k in range(planes)] + [core]).astype(jnp.int32)
    weight_up, weight_far = (
        pltpu.with_memory_space_constraint(w, pltpu.HBM) for w in (weight_up, weight_far)
    )
    weights = [weight, weight_up, weight_far, weight_down]
    own, other = mix(place, plane.reshape(-1, plane.shape[-1]), weights, drafts)

    tensors = lax.axis_size("tensor")
    swap = [(t, t ^ 1) for t in range(tensors)]
    own = (own.astype(F32) + lax.ppermute(other, "tensor", swap).astype(F32)).astype(BF16)
    total = None
    for k in range(planes):
        pairs = []
        for index in range(lenders * tensors):
            (source_y, z), source = divmod(index // tensors, column), index % tensors
            lender = (source // 2 + k) % planes * column + z
            pairs.append((index, lender * tensors + source_y * 2 + source % 2))
        piece = lax.ppermute(own[k], ("lender", "tensor"), pairs).astype(F32)
        total = piece if total is None else total + piece
    return total.astype(BF16)


def solution(mesh):
    in_specs = (
        P("lender", None, "tensor", None),
        P("lender", None, None),
        P("lender", None, None),
        P("tensor", None, None),
        P("tensor", None, None),
        P("tensor", "lender"),
        P(),
        P(),
    )
    out_specs = P("tensor", None, "lender")
    return jax.shard_map(body, mesh=mesh, in_specs=in_specs, out_specs=out_specs, check_vma=False)
```

```python
import functools
import math

import jax
import jax.numpy as jnp
from jax import lax
from jax.experimental import pallas as pl
from jax.experimental.pallas import tpu as pltpu
from jax.sharding import PartitionSpec as P

MSCALE_SQ = (0.1 * math.log(40.0) + 1.0) ** 2
NEG_FILL = -1e30
BF16 = jnp.bfloat16
F32 = jnp.float32
PARTS = 3


def live_tokens(slot_request, context_lengths, slot_tokens):
    lenders = slot_request.shape[0]
    owners = jnp.arange(context_lengths.shape[0], dtype=jnp.int32)
    lengths = jnp.sum(
        jnp.where(
            slot_request[:, :, None] == owners[None, None, :], context_lengths[None, None, :], 0
        ),
        axis=-1,
    )
    matching = slot_request[:, None, :] == slot_request[None, :, :]
    before = jnp.arange(lenders)[:, None] < jnp.arange(lenders)[None, :]
    slot_rank = jnp.sum(jnp.where(matching & before[:, :, None], 1, 0), axis=0)
    return jnp.clip(lengths - slot_tokens * slot_rank, 0, slot_tokens)


def pack_kernel(
    home_ref, slot_request_ref, queries_ref, out_ref, nope_ref, rope_ref, packed_ref, sems
):
    reqs, drafts, heads, width = queries_ref.shape
    nope = nope_ref.shape[-1]
    half = heads * drafts // 2
    for i in range(reqs):
        for s in range(drafts):
            x = queries_ref[i, s].astype(F32)
            nope_ref[pl.ds(s, heads, stride=drafts), :] = x[:, :nope]
            rope_ref[pl.ds(s, heads, stride=drafts), :] = x[:, nope:]
        rope = rope_ref[...]
        rope = jnp.concatenate([rope[:half], rope[half:]], 1)
        packed_ref[i] = jnp.concatenate([nope_ref[...], rope], 0).astype(BF16)
    home = home_ref[0]
    copies = [
        pltpu.make_async_copy(
            packed_ref.at[jnp.clip(slot_request_ref[d, home] - home * reqs, 0, reqs - 1)],
            out_ref.at[d],
            sems.at[d],
        )
        for d in range(out_ref.shape[0])
    ]
    for copy in copies:
        copy.start()
    for copy in copies:
        copy.wait()


def pack(home, slot_request, queries, nope):
    reqs, drafts, heads, width = queries.shape
    rows = heads * drafts
    smem = pl.BlockSpec(memory_space=pltpu.SMEM)
    vmem = pl.BlockSpec(memory_space=pltpu.VMEM)
    slots = slot_request.shape[0]
    return pl.pallas_call(
        pack_kernel,
        out_shape=pltpu.HBM((slots, rows + rows // 2, nope), BF16),
        in_specs=[smem, smem, vmem],
        out_specs=pl.BlockSpec(memory_space=pltpu.HBM),
        scratch_shapes=[
            pltpu.VMEM((rows, nope), F32),
            pltpu.VMEM((rows, width - nope), F32),
            pltpu.VMEM((reqs, rows + rows // 2, nope), BF16),
            pltpu.SemaphoreType.DMA((slots,)),
        ],
        name="pack",
    )(home, slot_request, queries)


def lend_kernel(
    scale,
    group,
    live_ref,
    arrived_ref,
    keys_ref,
    values_any,
    pool_any,
    out_any,
    out_ref,
    values_ref,
    pool_ref,
    query_ref,
    mean_ref,
    sems,
):
    slots, _, nope = arrived_ref.shape
    heads, _, latent = keys_ref.shape
    vhead = values_ref.shape[-1]
    rows, width = query_ref.shape[1:]
    drafts = rows // heads
    rope = width - latent
    tokens = pool_ref.shape[1]
    pair = 2 * drafts
    blocks = rows // 16
    trips = slots // group

    def pool_part(t):
        at = pl.ds(t * group, group)
        return pltpu.make_async_copy(pool_any.at[at], pool_ref.at[at], sems.at[t])

    def leaving(t):
        at = pl.ds(t * group, group)
        return pltpu.make_async_copy(out_ref.at[at], out_any.at[at], sems.at[trips + t])

    def project(at, count):
        for block in range(blocks):
            part = mean_ref[at : at + count, 16 * block : 16 * block + 16, :].astype(F32)
            done = []
            for half in range(16 // pair):
                rows_in = part[:, pair * half : pair * half + pair].reshape(count * pair, latent)
                h = 16 // drafts * block + 2 * half
                both = jnp.concatenate([values_ref[h], values_ref[h + 1]], 1)
                both = jnp.dot(rows_in.astype(BF16), both, preferred_element_type=F32)
                both = jnp.where(first[: count * pair], both[:, :vhead], both[:, vhead:])
                done.append(both.reshape(count, pair, vhead))
            done = jnp.concatenate(done, 1).astype(BF16)
            out_ref[at : at + count, 16 * block : 16 * block + 16, :] = done

    values_copy = pltpu.make_async_copy(values_any, values_ref, sems.at[2 * trips])
    for t in range(trips):
        pool_part(t).start()
    values_copy.start()

    first = lax.broadcasted_iota(jnp.int32, (slots * pair, 1), 0) % pair < drafts

    for block in range(blocks):
        part = arrived_ref[:, 16 * block : 16 * block + 16, :].astype(F32)
        done = []
        for half in range(16 // pair):
            rows_in = part[:, pair * half : pair * half + pair].reshape(slots * pair, nope)
            rows_in = rows_in.astype(BF16)
            h = 16 // drafts * block + 2 * half
            one = jnp.dot(rows_in, keys_ref[h], preferred_element_type=F32)
            two = jnp.dot(rows_in, keys_ref[h + 1], preferred_element_type=F32)
            done.append(jnp.where(first, one, two).reshape(slots, pair, latent))
        query_ref[:, 16 * block : 16 * block + 16, :latent] = jnp.concatenate(done, 1).astype(BF16)
    half_rows = rows // 2
    query_ref[:, :half_rows, latent:] = arrived_ref[:, rows : rows + half_rows, :rope]
    query_ref[:, half_rows:, latent:] = arrived_ref[:, rows : rows + half_rows, rope : 2 * rope]

    eye = lax.broadcasted_iota(jnp.int32, (rows, vhead), 0) == lax.broadcasted_iota(
        jnp.int32, (rows, vhead), 1
    )
    line = lax.broadcasted_iota(jnp.int32, (8, vhead), 0)
    token = lax.broadcasted_iota(jnp.int32, (rows, tokens), 1)

    for t in range(trips):
        pool_part(t).wait()
        ns = [t * group + k for k in range(group)]
        scores = [
            lax.dot_general(
                query_ref[n], pool_ref[n], (((1,), (1,)), ((), ())), preferred_element_type=F32
            )
            * scale
            for n in ns
        ]
        scores = [jnp.where(token < live_ref[n], x, NEG_FILL) for n, x in zip(ns, scores)]
        tops = [jnp.max(x, axis=1, keepdims=True) for x in scores]
        weights = [jnp.exp(x - top) for x, top in zip(scores, tops)]
        totals = [jnp.sum(x, axis=1, keepdims=True) for x in weights]
        weighted = [
            jnp.dot(x.astype(BF16), pool_ref[n, :, :latent], preferred_element_type=F32)
            for n, x in zip(ns, weights)
        ]
        for n, top, total, x in zip(ns, tops, totals, weighted):
            mean_ref[n] = (x * (1.0 / total)).astype(BF16)
            mass = jnp.sum(jnp.where(eye, top + jnp.log(total), 0.0), axis=0, keepdims=True)
            high = mass.astype(BF16).astype(F32)
            middle = (mass - high).astype(BF16).astype(F32)
            low = mass - high - middle
            parts = jnp.where(line == 0, high, jnp.where(line == 1, middle, low))
            out_ref[n, rows:, :] = jnp.where(line < PARTS, parts, 0.0).astype(BF16)
        if t % 2 == 1:
            if t == 1:
                values_copy.wait()
            project((t - 1) * group, 2 * group)
            leaving(t - 1).start()
            leaving(t).start()
    for t in range(trips):
        leaving(t).wait()


def lend(live, arrived, key_absorb, value_absorb, pool, scale, group=8):
    slots, _, width = pool.shape
    latent = key_absorb.shape[2]
    vhead = value_absorb.shape[-1]
    rows = arrived.shape[1] * 2 // 3
    vmem = pl.BlockSpec(memory_space=pltpu.VMEM)
    hbm = pl.BlockSpec(memory_space=pl.ANY)
    return pl.pallas_call(
        functools.partial(lend_kernel, scale, group),
        out_shape=pltpu.HBM((slots, rows + 8, vhead), BF16),
        in_specs=[pl.BlockSpec(memory_space=pltpu.SMEM), vmem, vmem, hbm, hbm],
        out_specs=pl.BlockSpec(memory_space=pltpu.HBM),
        scratch_shapes=[
            pltpu.VMEM((slots, rows + 8, vhead), BF16),
            pltpu.VMEM(value_absorb.shape, BF16),
            pltpu.VMEM(pool.shape, BF16),
            pltpu.VMEM((slots, rows, width), BF16),
            pltpu.VMEM((slots, rows, latent), BF16),
            pltpu.SemaphoreType.DMA((2 * (slots // group) + 1,)),
        ],
        compiler_params=pltpu.CompilerParams(vmem_limit_bytes=28 * 2**20),
        name="lend",
    )(
        live,
        arrived,
        key_absorb,
        pltpu.with_memory_space_constraint(value_absorb, pltpu.HBM),
        pltpu.with_memory_space_constraint(pool, pltpu.HBM),
    )


def settle_kernel(back_ref, local_ref, draft_scores_ref, draft_values_ref, out_ref, rows_ref, wide_ref):
    slots, _, vhead = back_ref.shape
    reqs, rows, drafts = draft_scores_ref.shape
    heads = rows // drafts
    mass = jnp.sum(back_ref[:, rows:, :].astype(F32), axis=1)
    mass = jnp.transpose(mass)[:rows]
    local = local_ref[...]
    for i in range(reqs):
        member = local == i
        draft = draft_scores_ref[i]
        own = jnp.where(member, mass, NEG_FILL)
        top = jnp.maximum(
            jnp.max(own, axis=1, keepdims=True), jnp.max(draft, axis=1, keepdims=True)
        )
        weight = jnp.where(member, jnp.exp(own - top), 0.0)
        draft = jnp.exp(draft - top)
        total = jnp.sum(weight, axis=1, keepdims=True) + jnp.sum(draft, axis=1, keepdims=True)
        value = jnp.zeros((rows, vhead), F32)
        for n in range(slots):
            value = value + weight[:, n : n + 1] * back_ref[n, :rows, :].astype(F32)
        for j in range(drafts):
            for s in range(drafts):
                wide_ref[pl.ds(j * rows + s, heads, stride=drafts), :] = draft_values_ref[i, j]
            value = value + draft[:, j : j + 1] * wide_ref[j * rows : (j + 1) * rows]
        value = value / total
        for h in range(heads):
            at = (h * reqs + i) * drafts
            rows_ref[at : at + drafts, :] = value[h * drafts : (h + 1) * drafts]
    size = reqs * drafts
    joined = jnp.concatenate([rows_ref[h * size : (h + 1) * size] for h in range(heads)], 1)
    joined = joined.astype(BF16)
    for n in range(out_ref.shape[0]):
        out_ref[n] = joined


def settle(back, local, draft_scores, draft_values, copies):
    _, _, vhead = back.shape
    reqs, rows, drafts = draft_scores.shape
    vmem = pl.BlockSpec(memory_space=pltpu.VMEM)
    return pl.pallas_call(
        settle_kernel,
        out_shape=jax.ShapeDtypeStruct((copies, reqs * drafts, rows // drafts * vhead), BF16),
        in_specs=[vmem] * 4,
        out_specs=vmem,
        scratch_shapes=[
            pltpu.VMEM((reqs * rows, vhead), F32),
            pltpu.VMEM((drafts * rows, vhead), F32),
        ],
        compiler_params=pltpu.CompilerParams(vmem_limit_bytes=8 * 2**20),
        name="settle",
    )(back, local, draft_scores, draft_values)


def mix_kernel(place_ref, rows_ref, *refs):
    weights, (own_ref, other_ref, late_ref, held_ref, sems) = refs[:-5], refs[-5:]
    blocks = held_ref.shape[0]
    late = {
        k: pltpu.make_async_copy(weights[k], late_ref.at[n], sems.at[n])
        for n, k in enumerate((1, 2))
    }
    for copy in late.values():
        copy.start()
    dot = functools.partial(
        lax.dot_general,
        dimension_numbers=(((1,), (1,)), ((), ())),
        preferred_element_type=F32,
    )
    for k in (0, 3, 1, 2):
        if k in late:
            late[k].wait()
        done = dot(rows_ref[...], late_ref[k - 1] if k in late else weights[k][...])
        held_ref[k] = done
    for n in range(blocks):
        out_ref = (own_ref, other_ref)[n * 2 // blocks]
        piece = held_ref[place_ref[n]]
        out_ref[n % (blocks // 2)] = piece.reshape(out_ref.shape[1:]).astype(BF16)


def mix(place, rows, weights, drafts):
    blocks = place.shape[0]
    features = weights[0].shape[0]
    vmem = pl.BlockSpec(memory_space=pltpu.VMEM)
    half = jax.ShapeDtypeStruct((blocks // 2, rows.shape[0] // drafts, drafts, features), BF16)
    return pl.pallas_call(
        mix_kernel,
        out_shape=[half, half],
        in_specs=[
            pl.BlockSpec(memory_space=pltpu.SMEM),
            vmem,
            *[pl.BlockSpec(memory_space=pl.ANY) if i in (1, 2) else vmem for i in range(blocks)],
        ],
        out_specs=[vmem, vmem],
        scratch_shapes=[
            pltpu.VMEM((2,) + weights[0].shape, BF16),
            pltpu.VMEM((blocks, rows.shape[0], features), F32),
            pltpu.SemaphoreType.DMA((2,)),
        ],
        compiler_params=pltpu.CompilerParams(vmem_limit_bytes=12 * 2**20),
        name="mix",
    )(place, rows, *weights)


def body(
    draft_queries,
    draft_latents,
    latent_pool,
    key_absorb,
    value_absorb,
    out_proj,
    slot_request,
    context_lengths,
):
    home = lax.axis_index("lender")
    reqs, drafts, heads, width = draft_queries.shape
    nope, latent = key_absorb.shape[1:]
    tokens = latent_pool.shape[1]
    rows = heads * drafts
    scale = width ** (-0.5) * MSCALE_SQ

    outgoing = pack(jnp.full((1,), home, jnp.int32), slot_request, draft_queries, nope)
    outgoing, slot_request, context_lengths, draft_queries, draft_latents, out_proj = (
        lax.optimization_barrier(
            (outgoing, slot_request, context_lengths, draft_queries, draft_latents, out_proj)
        )
    )
    arrived = lax.all_to_all(outgoing, "lender", split_axis=0, concat_axis=0, tiled=True)

    live_all = live_tokens(slot_request, context_lengths, tokens)
    live_here = lax.dynamic_slice_in_dim(live_all, home, 1, 0)[0]
    local = lax.dynamic_slice_in_dim(slot_request, home, 1, 1).reshape(1, -1) - home * reqs
    lenders, column = latent_pool.shape[0], 8
    planes = lenders // column
    up = [(l, (l - column) % lenders) for l in range(lenders)]
    down = [(l, (l + column) % lenders) for l in range(lenders)]
    weight = out_proj.T
    weight_up = lax.ppermute(weight, "lender", up)

    part = jnp.einsum(
        "ishc,hcl->ihsl", draft_queries[..., :nope], key_absorb, preferred_element_type=F32
    ).astype(BF16)
    own = jnp.concatenate([part, jnp.swapaxes(draft_queries[..., nope:], 1, 2)], -1)
    draft_scores = (
        jnp.einsum("ihsk,ijk->ihsj", own, draft_latents, preferred_element_type=F32) * scale
    )
    causal = jnp.arange(drafts)[:, None] >= jnp.arange(drafts)[None, :]
    draft_scores = jnp.where(causal, draft_scores, NEG_FILL).reshape(reqs, rows, drafts)
    draft_values = jnp.einsum(
        "ijl,hlc->ijhc", draft_latents[:, :, :latent], value_absorb, preferred_element_type=F32
    )
    arrived, live_here, local, draft_scores, draft_values = lax.optimization_barrier(
        (arrived, live_here, local, draft_scores, draft_values)
    )

    sending = lend(live_here, arrived, key_absorb, value_absorb, latent_pool, scale)
    sending, weight = lax.optimization_barrier((sending, weight))
    back = lax.all_to_all(sending, "lender", split_axis=0, concat_axis=0, tiled=True)
    weight_far = lax.ppermute(weight_up, "lender", up)
    weight_down = lax.ppermute(weight, "lender", down)

    copies = settle(back, local, draft_scores, draft_values, column)
    inner = [[column * y + z for z in range(column)] for y in range(planes)]
    plane = lax.all_to_all(
        copies, "lender", split_axis=0, concat_axis=0, tiled=True, axis_index_groups=inner
    )
    plane, weight_far, weight_down = lax.optimization_barrier((plane, weight_far, weight_down))
    y = home // column
    tensor = lax.axis_index("tensor")
    x, core = tensor // 2, tensor % 2
    turns = [core, core + 2, 1 - core, 3 - core]
    place = jnp.stack([(x + k - y) % planes for k in turns]).astype(jnp.int32)
    weight_up, weight_far = (
        pltpu.with_memory_space_constraint(w, pltpu.HBM) for w in (weight_up, weight_far)
    )
    weights = [weight, weight_up, weight_far, weight_down]
    own, other = mix(place, plane.reshape(-1, plane.shape[-1]), weights, drafts)

    tensors = lax.axis_size("tensor")
    swap = [(t, t ^ 1) for t in range(tensors)]
    own = (own.astype(F32) + lax.ppermute(other, "tensor", swap).astype(F32)).astype(BF16)
    total = None
    for j in range(planes // 2):
        pairs = []
        for index in range(lenders * tensors):
            (source_y, z), source = divmod(index // tensors, column), index % tensors
            lender = (source // 2 + source % 2 + 2 * j) % planes * column + z
            pairs.append((index, lender * tensors + source_y * 2 + source % 2))
        piece = lax.ppermute(own[j], ("lender", "tensor"), pairs).astype(F32)
        total = piece if total is None else total + piece
    half = total.shape[0] // 2
    mine = jnp.where(core == 0, total[:half], total[half:])
    theirs = jnp.where(core == 0, total[half:], total[:half])
    return (mine + lax.ppermute(theirs, "tensor", swap)).astype(BF16)


def solution(mesh):
    in_specs = (
        P("lender", None, "tensor", None),
        P("lender", None, None),
        P("lender", None, None),
        P("tensor", None, None),
        P("tensor", None, None),
        P("tensor", "lender"),
        P(),
        P(),
    )
    out_specs = P("tensor", None, "lender")
    return jax.shard_map(body, mesh=mesh, in_specs=in_specs, out_specs=out_specs, check_vma=False)
```

```python
import functools
import math

import jax
import jax.numpy as jnp
from jax import lax
from jax.experimental import pallas as pl
from jax.experimental.pallas import tpu as pltpu
from jax.sharding import PartitionSpec as P

MSCALE_SQ = (0.1 * math.log(40.0) + 1.0) ** 2
NEG_FILL = -1e30
BF16 = jnp.bfloat16
F32 = jnp.float32
PARTS = 3
TURN = (0, 2, 4, 6, 1, 3, 5, 7)


def in_turn(n):
    return n // len(TURN) * len(TURN) + TURN[n % len(TURN)]


def live_tokens(slot_request, context_lengths, slot_tokens):
    lenders = slot_request.shape[0]
    owners = jnp.arange(context_lengths.shape[0], dtype=jnp.int32)
    lengths = jnp.sum(
        jnp.where(
            slot_request[:, :, None] == owners[None, None, :], context_lengths[None, None, :], 0
        ),
        axis=-1,
    )
    matching = slot_request[:, None, :] == slot_request[None, :, :]
    before = jnp.arange(lenders)[:, None] < jnp.arange(lenders)[None, :]
    slot_rank = jnp.sum(jnp.where(matching & before[:, :, None], 1, 0), axis=0)
    return jnp.clip(lengths - slot_tokens * slot_rank, 0, slot_tokens)


def pack_kernel(
    home_ref, slot_request_ref, queries_ref, out_ref, nope_ref, rope_ref, packed_ref, sems
):
    reqs, drafts, heads, width = queries_ref.shape
    nope = nope_ref.shape[-1]
    half = heads * drafts // 2
    for i in range(reqs):
        for s in range(drafts):
            x = queries_ref[i, s].astype(F32)
            nope_ref[pl.ds(s, heads, stride=drafts), :] = x[:, :nope]
            rope_ref[pl.ds(s, heads, stride=drafts), :] = x[:, nope:]
        rope = rope_ref[...]
        rope = jnp.concatenate([rope[:half], rope[half:]], 1)
        packed_ref[i] = jnp.concatenate([nope_ref[...], rope], 0).astype(BF16)
    home = home_ref[0]
    copies = [
        pltpu.make_async_copy(
            packed_ref.at[
                jnp.clip(slot_request_ref[in_turn(d), home] - home * reqs, 0, reqs - 1)
            ],
            out_ref.at[d],
            sems.at[d],
        )
        for d in range(out_ref.shape[0])
    ]
    for copy in copies:
        copy.start()
    for copy in copies:
        copy.wait()


def pack(home, slot_request, queries, nope):
    reqs, drafts, heads, width = queries.shape
    rows = heads * drafts
    smem = pl.BlockSpec(memory_space=pltpu.SMEM)
    vmem = pl.BlockSpec(memory_space=pltpu.VMEM)
    slots = slot_request.shape[0]
    return pl.pallas_call(
        pack_kernel,
        out_shape=pltpu.HBM((slots, rows + rows // 2, nope), BF16),
        in_specs=[smem, smem, vmem],
        out_specs=pl.BlockSpec(memory_space=pltpu.HBM),
        scratch_shapes=[
            pltpu.VMEM((rows, nope), F32),
            pltpu.VMEM((rows, width - nope), F32),
            pltpu.VMEM((reqs, rows + rows // 2, nope), BF16),
            pltpu.SemaphoreType.DMA((slots,)),
        ],
        name="pack",
    )(home, slot_request, queries)


def lend_kernel(
    scale,
    group,
    live_ref,
    arrived_ref,
    keys_ref,
    values_any,
    pool_any,
    out_any,
    out_ref,
    values_ref,
    pool_ref,
    query_ref,
    mean_ref,
    sems,
):
    slots, _, nope = arrived_ref.shape
    heads, _, latent = keys_ref.shape
    vhead = values_ref.shape[-1]
    rows, width = query_ref.shape[1:]
    drafts = rows // heads
    rope = width - latent
    tokens = pool_ref.shape[1]
    pair = 2 * drafts
    blocks = rows // 16
    trips = slots // group

    def pool_part(t):
        at = pl.ds(t * group, group)
        return pltpu.make_async_copy(pool_any.at[at], pool_ref.at[at], sems.at[t])

    def leaving(t):
        at = pl.ds(t * group, group)
        return pltpu.make_async_copy(out_ref.at[at], out_any.at[at], sems.at[trips + t])

    def project(at, count):
        for block in range(blocks):
            part = mean_ref[at : at + count, 16 * block : 16 * block + 16, :].astype(F32)
            done = []
            for half in range(16 // pair):
                rows_in = part[:, pair * half : pair * half + pair].reshape(count * pair, latent)
                h = 16 // drafts * block + 2 * half
                both = jnp.concatenate([values_ref[h], values_ref[h + 1]], 1)
                both = jnp.dot(rows_in.astype(BF16), both, preferred_element_type=F32)
                both = jnp.where(first[: count * pair], both[:, :vhead], both[:, vhead:])
                done.append(both.reshape(count, pair, vhead))
            done = jnp.concatenate(done, 1).astype(BF16)
            out_ref[at : at + count, 16 * block : 16 * block + 16, :] = done

    values_copy = pltpu.make_async_copy(values_any, values_ref, sems.at[2 * trips])
    for t in range(trips):
        pool_part(t).start()
    values_copy.start()

    first = lax.broadcasted_iota(jnp.int32, (slots * pair, 1), 0) % pair < drafts

    for block in range(blocks):
        part = arrived_ref[:, 16 * block : 16 * block + 16, :].astype(F32)
        done = []
        for half in range(16 // pair):
            rows_in = part[:, pair * half : pair * half + pair].reshape(slots * pair, nope)
            rows_in = rows_in.astype(BF16)
            h = 16 // drafts * block + 2 * half
            one = jnp.dot(rows_in, keys_ref[h], preferred_element_type=F32)
            two = jnp.dot(rows_in, keys_ref[h + 1], preferred_element_type=F32)
            done.append(jnp.where(first, one, two).reshape(slots, pair, latent))
        query_ref[:, 16 * block : 16 * block + 16, :latent] = jnp.concatenate(done, 1).astype(BF16)
    half_rows = rows // 2
    query_ref[:, :half_rows, latent:] = arrived_ref[:, rows : rows + half_rows, :rope]
    query_ref[:, half_rows:, latent:] = arrived_ref[:, rows : rows + half_rows, rope : 2 * rope]

    eye = lax.broadcasted_iota(jnp.int32, (rows, vhead), 0) == lax.broadcasted_iota(
        jnp.int32, (rows, vhead), 1
    )
    line = lax.broadcasted_iota(jnp.int32, (8, vhead), 0)
    token = lax.broadcasted_iota(jnp.int32, (rows, tokens), 1)

    for t in range(trips):
        pool_part(t).wait()
        ns = [t * group + k for k in range(group)]
        scores = [
            lax.dot_general(
                query_ref[n],
                pool_ref[in_turn(n)],
                (((1,), (1,)), ((), ())),
                preferred_element_type=F32,
            )
            * scale
            for n in ns
        ]
        scores = [jnp.where(token < live_ref[in_turn(n)], x, NEG_FILL) for n, x in zip(ns, scores)]
        tops = [jnp.max(x, axis=1, keepdims=True) for x in scores]
        weights = [jnp.exp(x - top) for x, top in zip(scores, tops)]
        totals = [jnp.sum(x, axis=1, keepdims=True) for x in weights]
        weighted = [
            jnp.dot(x.astype(BF16), pool_ref[in_turn(n), :, :latent], preferred_element_type=F32)
            for n, x in zip(ns, weights)
        ]
        for n, top, total, x in zip(ns, tops, totals, weighted):
            mean_ref[n] = (x * (1.0 / total)).astype(BF16)
            mass = jnp.sum(jnp.where(eye, top + jnp.log(total), 0.0), axis=0, keepdims=True)
            high = mass.astype(BF16).astype(F32)
            middle = (mass - high).astype(BF16).astype(F32)
            low = mass - high - middle
            parts = jnp.where(line == 0, high, jnp.where(line == 1, middle, low))
            out_ref[n, rows:, :] = jnp.where(line < PARTS, parts, 0.0).astype(BF16)
        if t % 2 == 1:
            if t == 1:
                values_copy.wait()
            project((t - 1) * group, 2 * group)
            leaving(t - 1).start()
            leaving(t).start()
    for t in range(trips):
        leaving(t).wait()


def lend(live, arrived, key_absorb, value_absorb, pool, scale, group=8):
    slots, _, width = pool.shape
    latent = key_absorb.shape[2]
    vhead = value_absorb.shape[-1]
    rows = arrived.shape[1] * 2 // 3
    vmem = pl.BlockSpec(memory_space=pltpu.VMEM)
    hbm = pl.BlockSpec(memory_space=pl.ANY)
    return pl.pallas_call(
        functools.partial(lend_kernel, scale, group),
        out_shape=pltpu.HBM((slots, rows + 8, vhead), BF16),
        in_specs=[pl.BlockSpec(memory_space=pltpu.SMEM), vmem, vmem, hbm, hbm],
        out_specs=pl.BlockSpec(memory_space=pltpu.HBM),
        scratch_shapes=[
            pltpu.VMEM((slots, rows + 8, vhead), BF16),
            pltpu.VMEM(value_absorb.shape, BF16),
            pltpu.VMEM(pool.shape, BF16),
            pltpu.VMEM((slots, rows, width), BF16),
            pltpu.VMEM((slots, rows, latent), BF16),
            pltpu.SemaphoreType.DMA((2 * (slots // group) + 1,)),
        ],
        compiler_params=pltpu.CompilerParams(vmem_limit_bytes=28 * 2**20),
        name="lend",
    )(
        live,
        arrived,
        key_absorb,
        pltpu.with_memory_space_constraint(value_absorb, pltpu.HBM),
        pltpu.with_memory_space_constraint(pool, pltpu.HBM),
    )


def settle_kernel(back_ref, local_ref, draft_scores_ref, draft_values_ref, out_ref, rows_ref, wide_ref):
    slots, _, vhead = back_ref.shape
    reqs, rows, drafts = draft_scores_ref.shape
    heads = rows // drafts
    mass = jnp.sum(back_ref[:, rows:, :].astype(F32), axis=1)
    mass = jnp.transpose(mass)[:rows]
    local = local_ref[...]
    for i in range(reqs):
        member = local == i
        draft = draft_scores_ref[i]
        own = jnp.where(member, mass, NEG_FILL)
        top = jnp.maximum(
            jnp.max(own, axis=1, keepdims=True), jnp.max(draft, axis=1, keepdims=True)
        )
        weight = jnp.where(member, jnp.exp(own - top), 0.0)
        draft = jnp.exp(draft - top)
        total = jnp.sum(weight, axis=1, keepdims=True) + jnp.sum(draft, axis=1, keepdims=True)
        value = jnp.zeros((rows, vhead), F32)
        for n in range(slots):
            value = value + weight[:, n : n + 1] * back_ref[n, :rows, :].astype(F32)
        for j in range(drafts):
            for s in range(drafts):
                wide_ref[pl.ds(j * rows + s, heads, stride=drafts), :] = draft_values_ref[i, j]
            value = value + draft[:, j : j + 1] * wide_ref[j * rows : (j + 1) * rows]
        value = value / total
        for h in range(heads):
            at = (h * reqs + i) * drafts
            rows_ref[at : at + drafts, :] = value[h * drafts : (h + 1) * drafts]
    size = reqs * drafts
    joined = jnp.concatenate([rows_ref[h * size : (h + 1) * size] for h in range(heads)], 1)
    joined = joined.astype(BF16)
    for n in range(out_ref.shape[0]):
        out_ref[n] = joined


def settle(back, local, draft_scores, draft_values, copies):
    _, _, vhead = back.shape
    reqs, rows, drafts = draft_scores.shape
    vmem = pl.BlockSpec(memory_space=pltpu.VMEM)
    return pl.pallas_call(
        settle_kernel,
        out_shape=jax.ShapeDtypeStruct((copies, reqs * drafts, rows // drafts * vhead), BF16),
        in_specs=[vmem] * 4,
        out_specs=vmem,
        scratch_shapes=[
            pltpu.VMEM((reqs * rows, vhead), F32),
            pltpu.VMEM((drafts * rows, vhead), F32),
        ],
        compiler_params=pltpu.CompilerParams(vmem_limit_bytes=8 * 2**20),
        name="settle",
    )(back, local, draft_scores, draft_values)


def mix_kernel(place_ref, rows_ref, *refs):
    weights, (own_ref, other_ref, late_ref, held_ref, sems) = refs[:-5], refs[-5:]
    blocks = held_ref.shape[0]
    late = {
        k: pltpu.make_async_copy(weights[k], late_ref.at[n], sems.at[n])
        for n, k in enumerate((1, 2))
    }
    for copy in late.values():
        copy.start()
    dot = functools.partial(
        lax.dot_general,
        dimension_numbers=(((1,), (1,)), ((), ())),
        preferred_element_type=F32,
    )
    for k in (0, 3, 1, 2):
        if k in late:
            late[k].wait()
        done = dot(rows_ref[...], late_ref[k - 1] if k in late else weights[k][...])
        held_ref[k] = done
    for n in range(blocks):
        out_ref = (own_ref, other_ref)[n * 2 // blocks]
        piece = held_ref[place_ref[n]]
        out_ref[n % (blocks // 2)] = piece.reshape(out_ref.shape[1:]).astype(BF16)


def mix(place, rows, weights, drafts):
    blocks = place.shape[0]
    features = weights[0].shape[0]
    vmem = pl.BlockSpec(memory_space=pltpu.VMEM)
    half = jax.ShapeDtypeStruct((blocks // 2, rows.shape[0] // drafts, drafts, features), BF16)
    return pl.pallas_call(
        mix_kernel,
        out_shape=[half, half],
        in_specs=[
            pl.BlockSpec(memory_space=pltpu.SMEM),
            vmem,
            *[pl.BlockSpec(memory_space=pl.ANY) if i in (1, 2) else vmem for i in range(blocks)],
        ],
        out_specs=[vmem, vmem],
        scratch_shapes=[
            pltpu.VMEM((2,) + weights[0].shape, BF16),
            pltpu.VMEM((blocks, rows.shape[0], features), F32),
            pltpu.SemaphoreType.DMA((2,)),
        ],
        compiler_params=pltpu.CompilerParams(vmem_limit_bytes=12 * 2**20),
        name="mix",
    )(place, rows, *weights)


def body(
    draft_queries,
    draft_latents,
    latent_pool,
    key_absorb,
    value_absorb,
    out_proj,
    slot_request,
    context_lengths,
):
    home = lax.axis_index("lender")
    reqs, drafts, heads, width = draft_queries.shape
    nope, latent = key_absorb.shape[1:]
    tokens = latent_pool.shape[1]
    rows = heads * drafts
    scale = width ** (-0.5) * MSCALE_SQ

    outgoing = pack(jnp.full((1,), home, jnp.int32), slot_request, draft_queries, nope)
    outgoing, slot_request, context_lengths, draft_queries, draft_latents, out_proj = (
        lax.optimization_barrier(
            (outgoing, slot_request, context_lengths, draft_queries, draft_latents, out_proj)
        )
    )
    slots = latent_pool.shape[0]
    turn = [in_turn(n) for n in range(slots)]
    arrived = lax.all_to_all(
        outgoing, "lender", split_axis=0, concat_axis=0, tiled=True, axis_index_groups=[turn]
    )

    live_all = live_tokens(slot_request, context_lengths, tokens)
    live_here = lax.dynamic_slice_in_dim(live_all, home, 1, 0)[0]
    local = lax.dynamic_slice_in_dim(slot_request, home, 1, 1)[:, 0] - home * reqs
    local = local.reshape(-1, len(TURN) // 2, 2)
    local = jnp.concatenate([local[:, :, 0], local[:, :, 1]], axis=1).reshape(1, -1)
    lenders, column = latent_pool.shape[0], 8
    planes = lenders // column
    up = [(l, (l - column) % lenders) for l in range(lenders)]
    down = [(l, (l + column) % lenders) for l in range(lenders)]
    weight = out_proj.T
    weight_up = lax.ppermute(weight, "lender", up)

    part = jnp.einsum(
        "ishc,hcl->ihsl", draft_queries[..., :nope], key_absorb, preferred_element_type=F32
    ).astype(BF16)
    own = jnp.concatenate([part, jnp.swapaxes(draft_queries[..., nope:], 1, 2)], -1)
    draft_scores = (
        jnp.einsum("ihsk,ijk->ihsj", own, draft_latents, preferred_element_type=F32) * scale
    )
    causal = jnp.arange(drafts)[:, None] >= jnp.arange(drafts)[None, :]
    draft_scores = jnp.where(causal, draft_scores, NEG_FILL).reshape(reqs, rows, drafts)
    draft_values = jnp.einsum(
        "ijl,hlc->ijhc", draft_latents[:, :, :latent], value_absorb, preferred_element_type=F32
    )
    arrived, live_here, local, draft_scores, draft_values = lax.optimization_barrier(
        (arrived, live_here, local, draft_scores, draft_values)
    )

    sending = lend(live_here, arrived, key_absorb, value_absorb, latent_pool, scale)
    sending, weight = lax.optimization_barrier((sending, weight))
    back = lax.all_to_all(
        sending, "lender", split_axis=0, concat_axis=0, tiled=True, axis_index_groups=[turn]
    )
    weight_far = lax.ppermute(weight_up, "lender", up)
    weight_down = lax.ppermute(weight, "lender", down)

    copies = settle(back, local, draft_scores, draft_values, column)
    inner = [[column * y + z for z in range(column)] for y in range(planes)]
    plane = lax.all_to_all(
        copies, "lender", split_axis=0, concat_axis=0, tiled=True, axis_index_groups=inner
    )
    plane, weight_far, weight_down = lax.optimization_barrier((plane, weight_far, weight_down))
    y = home // column
    tensor = lax.axis_index("tensor")
    x, core = tensor // 2, tensor % 2
    turns = [core, core + 2, 1 - core, 3 - core]
    place = jnp.stack([(x + k - y) % planes for k in turns]).astype(jnp.int32)
    weight_up, weight_far = (
        pltpu.with_memory_space_constraint(w, pltpu.HBM) for w in (weight_up, weight_far)
    )
    weights = [weight, weight_up, weight_far, weight_down]
    own, other = mix(place, plane.reshape(-1, plane.shape[-1]), weights, drafts)

    tensors = lax.axis_size("tensor")
    swap = [(t, t ^ 1) for t in range(tensors)]
    own = (own.astype(F32) + lax.ppermute(other, "tensor", swap).astype(F32)).astype(BF16)
    total = None
    for j in range(planes // 2):
        pairs = []
        for index in range(lenders * tensors):
            (source_y, z), source = divmod(index // tensors, column), index % tensors
            lender = (source // 2 + source % 2 + 2 * j) % planes * column + z
            pairs.append((index, lender * tensors + source_y * 2 + source % 2))
        piece = lax.ppermute(own[j], ("lender", "tensor"), pairs).astype(F32)
        total = piece if total is None else total + piece
    half = total.shape[0] // 2
    mine = jnp.where(core == 0, total[:half], total[half:])
    theirs = jnp.where(core == 0, total[half:], total[:half])
    return (mine + lax.ppermute(theirs, "tensor", swap)).astype(BF16)


def solution(mesh):
    in_specs = (
        P("lender", None, "tensor", None),
        P("lender", None, None),
        P("lender", None, None),
        P("tensor", None, None),
        P("tensor", None, None),
        P("tensor", "lender"),
        P(),
        P(),
    )
    out_specs = P("tensor", None, "lender")
    return jax.shard_map(body, mesh=mesh, in_specs=in_specs, out_specs=out_specs, check_vma=False)
```

```python
import functools
import math

import jax
import jax.numpy as jnp
from jax import lax
from jax.experimental import pallas as pl
from jax.experimental.pallas import tpu as pltpu
from jax.sharding import PartitionSpec as P

MSCALE_SQ = (0.1 * math.log(40.0) + 1.0) ** 2
NEG_FILL = -1e30
BF16 = jnp.bfloat16
F32 = jnp.float32
PARTS = 3
TURN = (0, 2, 4, 6, 1, 3, 5, 7)


def in_turn(n):
    return n // len(TURN) * len(TURN) + TURN[n % len(TURN)]


def live_tokens(slot_request, context_lengths, slot_tokens):
    lenders = slot_request.shape[0]
    owners = jnp.arange(context_lengths.shape[0], dtype=jnp.int32)
    lengths = jnp.sum(
        jnp.where(
            slot_request[:, :, None] == owners[None, None, :], context_lengths[None, None, :], 0
        ),
        axis=-1,
    )
    matching = slot_request[:, None, :] == slot_request[None, :, :]
    before = jnp.arange(lenders)[:, None] < jnp.arange(lenders)[None, :]
    slot_rank = jnp.sum(jnp.where(matching & before[:, :, None], 1, 0), axis=0)
    return jnp.clip(lengths - slot_tokens * slot_rank, 0, slot_tokens)


def pack_kernel(
    home_ref, slot_request_ref, queries_ref, out_ref, nope_ref, rope_ref, packed_ref, sems
):
    reqs, drafts, heads, width = queries_ref.shape
    nope = nope_ref.shape[-1]
    half = heads * drafts // 2
    for i in range(reqs):
        for s in range(drafts):
            x = queries_ref[i, s].astype(F32)
            nope_ref[pl.ds(s, heads, stride=drafts), :] = x[:, :nope]
            rope_ref[pl.ds(s, heads, stride=drafts), :] = x[:, nope:]
        rope = rope_ref[...]
        rope = jnp.concatenate([rope[:half], rope[half:]], 1)
        packed_ref[i] = jnp.concatenate([nope_ref[...], rope], 0).astype(BF16)
    home = home_ref[0]
    copies = [
        pltpu.make_async_copy(
            packed_ref.at[
                jnp.clip(slot_request_ref[in_turn(d), home] - home * reqs, 0, reqs - 1)
            ],
            out_ref.at[d],
            sems.at[d],
        )
        for d in range(out_ref.shape[0])
    ]
    for copy in copies:
        copy.start()
    for copy in copies:
        copy.wait()


def pack(home, slot_request, queries, nope):
    reqs, drafts, heads, width = queries.shape
    rows = heads * drafts
    smem = pl.BlockSpec(memory_space=pltpu.SMEM)
    vmem = pl.BlockSpec(memory_space=pltpu.VMEM)
    slots = slot_request.shape[0]
    return pl.pallas_call(
        pack_kernel,
        out_shape=pltpu.HBM((slots, rows + rows // 2, nope), BF16),
        in_specs=[smem, smem, vmem],
        out_specs=pl.BlockSpec(memory_space=pltpu.HBM),
        scratch_shapes=[
            pltpu.VMEM((rows, nope), F32),
            pltpu.VMEM((rows, width - nope), F32),
            pltpu.VMEM((reqs, rows + rows // 2, nope), BF16),
            pltpu.SemaphoreType.DMA((slots,)),
        ],
        name="pack",
    )(home, slot_request, queries)


def lend_kernel(
    scale,
    group,
    live_ref,
    arrived_ref,
    keys_ref,
    values_any,
    pool_any,
    out_any,
    out_ref,
    values_ref,
    pool_ref,
    query_ref,
    mean_ref,
    sems,
):
    slots, _, nope = arrived_ref.shape
    heads, _, latent = keys_ref.shape
    vhead = values_ref.shape[-1]
    rows, width = query_ref.shape[1:]
    drafts = rows // heads
    rope = width - latent
    tokens = pool_ref.shape[1]
    pair = 2 * drafts
    blocks = rows // 16
    trips = slots // group

    def pool_part(t):
        at = pl.ds(t * group, group)
        return pltpu.make_async_copy(pool_any.at[at], pool_ref.at[at], sems.at[t])

    def leaving(t):
        at = pl.ds(t * group, group)
        return pltpu.make_async_copy(out_ref.at[at], out_any.at[at], sems.at[trips + t])

    def project(at, count):
        for block in range(blocks):
            part = mean_ref[at : at + count, 16 * block : 16 * block + 16, :].astype(F32)
            done = []
            for half in range(16 // pair):
                rows_in = part[:, pair * half : pair * half + pair].reshape(count * pair, latent)
                h = 16 // drafts * block + 2 * half
                both = jnp.concatenate([values_ref[h], values_ref[h + 1]], 1)
                both = jnp.dot(rows_in.astype(BF16), both, preferred_element_type=F32)
                both = jnp.where(first[: count * pair], both[:, :vhead], both[:, vhead:])
                done.append(both.reshape(count, pair, vhead))
            done = jnp.concatenate(done, 1).astype(BF16)
            out_ref[at : at + count, 16 * block : 16 * block + 16, :] = done

    values_copy = pltpu.make_async_copy(values_any, values_ref, sems.at[2 * trips])
    for t in range(trips):
        pool_part(t).start()
    values_copy.start()

    first = lax.broadcasted_iota(jnp.int32, (slots * pair, 1), 0) % pair < drafts

    for block in range(blocks):
        part = arrived_ref[:, 16 * block : 16 * block + 16, :].astype(F32)
        done = []
        for half in range(16 // pair):
            rows_in = part[:, pair * half : pair * half + pair].reshape(slots * pair, nope)
            rows_in = rows_in.astype(BF16)
            h = 16 // drafts * block + 2 * half
            one = jnp.dot(rows_in, keys_ref[h], preferred_element_type=F32)
            two = jnp.dot(rows_in, keys_ref[h + 1], preferred_element_type=F32)
            done.append(jnp.where(first, one, two).reshape(slots, pair, latent))
        query_ref[:, 16 * block : 16 * block + 16, :latent] = jnp.concatenate(done, 1).astype(BF16)
    half_rows = rows // 2
    query_ref[:, :half_rows, latent:] = arrived_ref[:, rows : rows + half_rows, :rope]
    query_ref[:, half_rows:, latent:] = arrived_ref[:, rows : rows + half_rows, rope : 2 * rope]

    eye = lax.broadcasted_iota(jnp.int32, (rows, vhead), 0) == lax.broadcasted_iota(
        jnp.int32, (rows, vhead), 1
    )
    line = lax.broadcasted_iota(jnp.int32, (8, vhead), 0)
    token = lax.broadcasted_iota(jnp.int32, (rows, tokens), 1)

    for t in range(trips):
        pool_part(t).wait()
        ns = [t * group + k for k in range(group)]
        scores = [
            lax.dot_general(
                query_ref[n],
                pool_ref[in_turn(n)],
                (((1,), (1,)), ((), ())),
                preferred_element_type=F32,
            )
            * scale
            for n in ns
        ]
        scores = [jnp.where(token < live_ref[in_turn(n)], x, NEG_FILL) for n, x in zip(ns, scores)]
        tops = [jnp.max(x, axis=1, keepdims=True) for x in scores]
        weights = [jnp.exp(x - top) for x, top in zip(scores, tops)]
        totals = [jnp.sum(x, axis=1, keepdims=True) for x in weights]
        weighted = [
            jnp.dot(x.astype(BF16), pool_ref[in_turn(n), :, :latent], preferred_element_type=F32)
            for n, x in zip(ns, weights)
        ]
        for n, top, total, x in zip(ns, tops, totals, weighted):
            mean_ref[n] = (x * (1.0 / total)).astype(BF16)
            mass = jnp.sum(jnp.where(eye, top + jnp.log(total), 0.0), axis=0, keepdims=True)
            high = mass.astype(BF16).astype(F32)
            middle = (mass - high).astype(BF16).astype(F32)
            low = mass - high - middle
            parts = jnp.where(line == 0, high, jnp.where(line == 1, middle, low))
            out_ref[n, rows:, :] = jnp.where(line < PARTS, parts, 0.0).astype(BF16)
        if t % 2 == 1:
            if t == 1:
                values_copy.wait()
            project((t - 1) * group, 2 * group)
            leaving(t - 1).start()
            leaving(t).start()
    for t in range(trips):
        leaving(t).wait()


def lend(live, arrived, key_absorb, value_absorb, pool, scale, group=8):
    slots, _, width = pool.shape
    latent = key_absorb.shape[2]
    vhead = value_absorb.shape[-1]
    rows = arrived.shape[1] * 2 // 3
    vmem = pl.BlockSpec(memory_space=pltpu.VMEM)
    hbm = pl.BlockSpec(memory_space=pl.ANY)
    return pl.pallas_call(
        functools.partial(lend_kernel, scale, group),
        out_shape=pltpu.HBM((slots, rows + 8, vhead), BF16),
        in_specs=[pl.BlockSpec(memory_space=pltpu.SMEM), vmem, vmem, hbm, hbm],
        out_specs=pl.BlockSpec(memory_space=pltpu.HBM),
        scratch_shapes=[
            pltpu.VMEM((slots, rows + 8, vhead), BF16),
            pltpu.VMEM(value_absorb.shape, BF16),
            pltpu.VMEM(pool.shape, BF16),
            pltpu.VMEM((slots, rows, width), BF16),
            pltpu.VMEM((slots, rows, latent), BF16),
            pltpu.SemaphoreType.DMA((2 * (slots // group) + 1,)),
        ],
        compiler_params=pltpu.CompilerParams(vmem_limit_bytes=28 * 2**20),
        name="lend",
    )(
        live,
        arrived,
        key_absorb,
        pltpu.with_memory_space_constraint(value_absorb, pltpu.HBM),
        pltpu.with_memory_space_constraint(pool, pltpu.HBM),
    )


def settle_kernel(back_ref, local_ref, draft_scores_ref, draft_values_ref, out_ref, rows_ref, wide_ref):
    slots, _, vhead = back_ref.shape
    reqs, rows, drafts = draft_scores_ref.shape
    heads = rows // drafts
    mass = jnp.sum(back_ref[:, rows:, :].astype(F32), axis=1)
    mass = jnp.transpose(mass)[:rows]
    local = local_ref[...]
    for i in range(reqs):
        member = local == i
        draft = draft_scores_ref[i]
        own = jnp.where(member, mass, NEG_FILL)
        top = jnp.maximum(
            jnp.max(own, axis=1, keepdims=True), jnp.max(draft, axis=1, keepdims=True)
        )
        weight = jnp.where(member, jnp.exp(own - top), 0.0)
        draft = jnp.exp(draft - top)
        total = jnp.sum(weight, axis=1, keepdims=True) + jnp.sum(draft, axis=1, keepdims=True)
        value = jnp.zeros((rows, vhead), F32)
        for n in range(slots):
            value = value + weight[:, n : n + 1] * back_ref[n, :rows, :].astype(F32)
        for j in range(drafts):
            for s in range(drafts):
                wide_ref[pl.ds(j * rows + s, heads, stride=drafts), :] = draft_values_ref[i, j]
            value = value + draft[:, j : j + 1] * wide_ref[j * rows : (j + 1) * rows]
        value = value / total
        for h in range(heads):
            at = (h * reqs + i) * drafts
            rows_ref[at : at + drafts, :] = value[h * drafts : (h + 1) * drafts]
    size = reqs * drafts
    joined = jnp.concatenate([rows_ref[h * size : (h + 1) * size] for h in range(heads)], 1)
    joined = joined.astype(BF16)
    for n in range(out_ref.shape[0]):
        out_ref[n] = joined


def settle(back, local, draft_scores, draft_values, copies):
    _, _, vhead = back.shape
    reqs, rows, drafts = draft_scores.shape
    vmem = pl.BlockSpec(memory_space=pltpu.VMEM)
    return pl.pallas_call(
        settle_kernel,
        out_shape=jax.ShapeDtypeStruct((copies, reqs * drafts, rows // drafts * vhead), BF16),
        in_specs=[vmem] * 4,
        out_specs=vmem,
        scratch_shapes=[
            pltpu.VMEM((reqs * rows, vhead), F32),
            pltpu.VMEM((drafts * rows, vhead), F32),
        ],
        compiler_params=pltpu.CompilerParams(vmem_limit_bytes=8 * 2**20),
        name="settle",
    )(back, local, draft_scores, draft_values)


def mix_kernel(place_ref, rows_ref, *refs):
    weights, (own_ref, other_ref, late_ref, held_ref, sems) = refs[:-5], refs[-5:]
    blocks = held_ref.shape[0]
    late = {
        k: pltpu.make_async_copy(weights[k], late_ref.at[n], sems.at[n])
        for n, k in enumerate((1, 2))
    }
    for copy in late.values():
        copy.start()
    dot = functools.partial(
        lax.dot_general,
        dimension_numbers=(((1,), (1,)), ((), ())),
        preferred_element_type=F32,
    )
    for k in (0, 3, 1, 2):
        if k in late:
            late[k].wait()
        done = dot(rows_ref[...], late_ref[k - 1] if k in late else weights[k][...])
        held_ref[k] = done
    for n in range(blocks):
        out_ref = (own_ref, other_ref)[n * 2 // blocks]
        piece = held_ref[place_ref[n]]
        size = piece.shape[0] // len(TURN)
        places = [TURN.index(z) * size for z in range(len(TURN))]
        piece = jnp.concatenate([piece[at : at + size] for at in places])
        out_ref[n % (blocks // 2)] = piece.reshape(out_ref.shape[1:]).astype(BF16)


def mix(place, rows, weights, drafts):
    blocks = place.shape[0]
    features = weights[0].shape[0]
    vmem = pl.BlockSpec(memory_space=pltpu.VMEM)
    half = jax.ShapeDtypeStruct((blocks // 2, rows.shape[0] // drafts, drafts, features), BF16)
    return pl.pallas_call(
        mix_kernel,
        out_shape=[half, half],
        in_specs=[
            pl.BlockSpec(memory_space=pltpu.SMEM),
            vmem,
            *[pl.BlockSpec(memory_space=pl.ANY) if i in (1, 2) else vmem for i in range(blocks)],
        ],
        out_specs=[vmem, vmem],
        scratch_shapes=[
            pltpu.VMEM((2,) + weights[0].shape, BF16),
            pltpu.VMEM((blocks, rows.shape[0], features), F32),
            pltpu.SemaphoreType.DMA((2,)),
        ],
        compiler_params=pltpu.CompilerParams(vmem_limit_bytes=12 * 2**20),
        name="mix",
    )(place, rows, *weights)


def body(
    draft_queries,
    draft_latents,
    latent_pool,
    key_absorb,
    value_absorb,
    out_proj,
    slot_request,
    context_lengths,
):
    home = lax.axis_index("lender")
    reqs, drafts, heads, width = draft_queries.shape
    nope, latent = key_absorb.shape[1:]
    tokens = latent_pool.shape[1]
    rows = heads * drafts
    scale = width ** (-0.5) * MSCALE_SQ

    outgoing = pack(jnp.full((1,), home, jnp.int32), slot_request, draft_queries, nope)
    outgoing, slot_request, context_lengths, draft_queries, draft_latents, out_proj = (
        lax.optimization_barrier(
            (outgoing, slot_request, context_lengths, draft_queries, draft_latents, out_proj)
        )
    )
    slots = latent_pool.shape[0]
    turn = [in_turn(n) for n in range(slots)]
    arrived = lax.all_to_all(
        outgoing, "lender", split_axis=0, concat_axis=0, tiled=True, axis_index_groups=[turn]
    )

    live_all = live_tokens(slot_request, context_lengths, tokens)
    live_here = lax.dynamic_slice_in_dim(live_all, home, 1, 0)[0]
    local = lax.dynamic_slice_in_dim(slot_request, home, 1, 1)[:, 0] - home * reqs
    local = local.reshape(-1, len(TURN) // 2, 2)
    local = jnp.concatenate([local[:, :, 0], local[:, :, 1]], axis=1).reshape(1, -1)
    lenders, column = latent_pool.shape[0], 8
    planes = lenders // column
    up = [(l, (l - column) % lenders) for l in range(lenders)]
    down = [(l, (l + column) % lenders) for l in range(lenders)]
    weight = out_proj.T
    weight_up = lax.ppermute(weight, "lender", up)

    part = jnp.einsum(
        "ishc,hcl->ihsl", draft_queries[..., :nope], key_absorb, preferred_element_type=F32
    ).astype(BF16)
    own = jnp.concatenate([part, jnp.swapaxes(draft_queries[..., nope:], 1, 2)], -1)
    draft_scores = (
        jnp.einsum("ihsk,ijk->ihsj", own, draft_latents, preferred_element_type=F32) * scale
    )
    causal = jnp.arange(drafts)[:, None] >= jnp.arange(drafts)[None, :]
    draft_scores = jnp.where(causal, draft_scores, NEG_FILL).reshape(reqs, rows, drafts)
    draft_values = jnp.einsum(
        "ijl,hlc->ijhc", draft_latents[:, :, :latent], value_absorb, preferred_element_type=F32
    )
    arrived, live_here, local, draft_scores, draft_values = lax.optimization_barrier(
        (arrived, live_here, local, draft_scores, draft_values)
    )

    sending = lend(live_here, arrived, key_absorb, value_absorb, latent_pool, scale)
    sending, weight = lax.optimization_barrier((sending, weight))
    back = lax.all_to_all(
        sending, "lender", split_axis=0, concat_axis=0, tiled=True, axis_index_groups=[turn]
    )
    weight_far = lax.ppermute(weight_up, "lender", up)
    weight_down = lax.ppermute(weight, "lender", down)

    copies = settle(back, local, draft_scores, draft_values, column)
    inner = [[in_turn(column * y + z) for z in range(column)] for y in range(planes)]
    plane = lax.all_to_all(
        copies, "lender", split_axis=0, concat_axis=0, tiled=True, axis_index_groups=inner
    )
    plane, weight_far, weight_down = lax.optimization_barrier((plane, weight_far, weight_down))
    y = home // column
    tensor = lax.axis_index("tensor")
    x, core = tensor // 2, tensor % 2
    turns = [core, core + 2, 1 - core, 3 - core]
    place = jnp.stack([(x + k - y) % planes for k in turns]).astype(jnp.int32)
    weight_up, weight_far = (
        pltpu.with_memory_space_constraint(w, pltpu.HBM) for w in (weight_up, weight_far)
    )
    weights = [weight, weight_up, weight_far, weight_down]
    own, other = mix(place, plane.reshape(-1, plane.shape[-1]), weights, drafts)

    tensors = lax.axis_size("tensor")
    swap = [(t, t ^ 1) for t in range(tensors)]
    own = (own.astype(F32) + lax.ppermute(other, "tensor", swap).astype(F32)).astype(BF16)
    total = None
    for j in range(planes // 2):
        pairs = []
        for index in range(lenders * tensors):
            (source_y, z), source = divmod(index // tensors, column), index % tensors
            lender = (source // 2 + source % 2 + 2 * j) % planes * column + z
            pairs.append((index, lender * tensors + source_y * 2 + source % 2))
        piece = lax.ppermute(own[j], ("lender", "tensor"), pairs).astype(F32)
        total = piece if total is None else total + piece
    half = total.shape[0] // 2
    mine = jnp.where(core == 0, total[:half], total[half:])
    theirs = jnp.where(core == 0, total[half:], total[:half])
    return (mine + lax.ppermute(theirs, "tensor", swap)).astype(BF16)


def solution(mesh):
    in_specs = (
        P("lender", None, "tensor", None),
        P("lender", None, None),
        P("lender", None, None),
        P("tensor", None, None),
        P("tensor", None, None),
        P("tensor", "lender"),
        P(),
        P(),
    )
    out_specs = P("tensor", None, "lender")
    return jax.shard_map(body, mesh=mesh, in_specs=in_specs, out_specs=out_specs, check_vma=False)
```

```python
import functools
import math

import jax
import jax.numpy as jnp
from jax import lax
from jax.experimental import pallas as pl
from jax.experimental.pallas import tpu as pltpu
from jax.sharding import PartitionSpec as P

MSCALE_SQ = (0.1 * math.log(40.0) + 1.0) ** 2
NEG_FILL = -1e30
BF16 = jnp.bfloat16
F32 = jnp.float32
PARTS = 3
TURN = (0, 4, 2, 6, 1, 5, 3, 7)


def in_turn(n):
    return n // len(TURN) * len(TURN) + TURN[n % len(TURN)]


def live_tokens(slot_request, context_lengths, slot_tokens):
    lenders = slot_request.shape[0]
    owners = jnp.arange(context_lengths.shape[0], dtype=jnp.int32)
    lengths = jnp.sum(
        jnp.where(
            slot_request[:, :, None] == owners[None, None, :], context_lengths[None, None, :], 0
        ),
        axis=-1,
    )
    matching = slot_request[:, None, :] == slot_request[None, :, :]
    before = jnp.arange(lenders)[:, None] < jnp.arange(lenders)[None, :]
    slot_rank = jnp.sum(jnp.where(matching & before[:, :, None], 1, 0), axis=0)
    return jnp.clip(lengths - slot_tokens * slot_rank, 0, slot_tokens)


def pack_kernel(
    home_ref, slot_request_ref, queries_ref, out_ref, nope_ref, rope_ref, packed_ref, sems
):
    reqs, drafts, heads, width = queries_ref.shape
    nope = nope_ref.shape[-1]
    half = heads * drafts // 2
    for i in range(reqs):
        for s in range(drafts):
            x = queries_ref[i, s].astype(F32)
            nope_ref[pl.ds(s, heads, stride=drafts), :] = x[:, :nope]
            rope_ref[pl.ds(s, heads, stride=drafts), :] = x[:, nope:]
        rope = rope_ref[...]
        rope = jnp.concatenate([rope[:half], rope[half:]], 1)
        packed_ref[i] = jnp.concatenate([nope_ref[...], rope], 0).astype(BF16)
    home = home_ref[0]
    copies = [
        pltpu.make_async_copy(
            packed_ref.at[
                jnp.clip(slot_request_ref[in_turn(d), home] - home * reqs, 0, reqs - 1)
            ],
            out_ref.at[d],
            sems.at[d],
        )
        for d in range(out_ref.shape[0])
    ]
    for copy in copies:
        copy.start()
    for copy in copies:
        copy.wait()


def pack(home, slot_request, queries, nope):
    reqs, drafts, heads, width = queries.shape
    rows = heads * drafts
    smem = pl.BlockSpec(memory_space=pltpu.SMEM)
    vmem = pl.BlockSpec(memory_space=pltpu.VMEM)
    slots = slot_request.shape[0]
    return pl.pallas_call(
        pack_kernel,
        out_shape=pltpu.HBM((slots, rows + rows // 2, nope), BF16),
        in_specs=[smem, smem, vmem],
        out_specs=pl.BlockSpec(memory_space=pltpu.HBM),
        scratch_shapes=[
            pltpu.VMEM((rows, nope), F32),
            pltpu.VMEM((rows, width - nope), F32),
            pltpu.VMEM((reqs, rows + rows // 2, nope), BF16),
            pltpu.SemaphoreType.DMA((slots,)),
        ],
        name="pack",
    )(home, slot_request, queries)


def lend_kernel(
    scale,
    group,
    live_ref,
    arrived_ref,
    keys_ref,
    values_any,
    pool_any,
    out_any,
    out_ref,
    values_ref,
    pool_ref,
    query_ref,
    mean_ref,
    sems,
):
    slots, _, nope = arrived_ref.shape
    heads, _, latent = keys_ref.shape
    vhead = values_ref.shape[-1]
    rows, width = query_ref.shape[1:]
    drafts = rows // heads
    rope = width - latent
    tokens = pool_ref.shape[1]
    pair = 2 * drafts
    blocks = rows // 16
    trips = slots // group

    def pool_part(t):
        at = pl.ds(t * group, group)
        return pltpu.make_async_copy(pool_any.at[at], pool_ref.at[at], sems.at[t])

    def leaving(t):
        at = pl.ds(t * group, group)
        return pltpu.make_async_copy(out_ref.at[at], out_any.at[at], sems.at[trips + t])

    def project(at, count):
        for block in range(blocks):
            part = mean_ref[at : at + count, 16 * block : 16 * block + 16, :].astype(F32)
            done = []
            for half in range(16 // pair):
                rows_in = part[:, pair * half : pair * half + pair].reshape(count * pair, latent)
                h = 16 // drafts * block + 2 * half
                both = jnp.concatenate([values_ref[h], values_ref[h + 1]], 1)
                both = jnp.dot(rows_in.astype(BF16), both, preferred_element_type=F32)
                both = jnp.where(first[: count * pair], both[:, :vhead], both[:, vhead:])
                done.append(both.reshape(count, pair, vhead))
            done = jnp.concatenate(done, 1).astype(BF16)
            out_ref[at : at + count, 16 * block : 16 * block + 16, :] = done

    values_copy = pltpu.make_async_copy(values_any, values_ref, sems.at[2 * trips])
    for t in range(trips):
        pool_part(t).start()
    values_copy.start()

    first = lax.broadcasted_iota(jnp.int32, (slots * pair, 1), 0) % pair < drafts

    for block in range(blocks):
        part = arrived_ref[:, 16 * block : 16 * block + 16, :].astype(F32)
        done = []
        for half in range(16 // pair):
            rows_in = part[:, pair * half : pair * half + pair].reshape(slots * pair, nope)
            rows_in = rows_in.astype(BF16)
            h = 16 // drafts * block + 2 * half
            one = jnp.dot(rows_in, keys_ref[h], preferred_element_type=F32)
            two = jnp.dot(rows_in, keys_ref[h + 1], preferred_element_type=F32)
            done.append(jnp.where(first, one, two).reshape(slots, pair, latent))
        query_ref[:, 16 * block : 16 * block + 16, :latent] = jnp.concatenate(done, 1).astype(BF16)
    half_rows = rows // 2
    query_ref[:, :half_rows, latent:] = arrived_ref[:, rows : rows + half_rows, :rope]
    query_ref[:, half_rows:, latent:] = arrived_ref[:, rows : rows + half_rows, rope : 2 * rope]

    eye = lax.broadcasted_iota(jnp.int32, (rows, vhead), 0) == lax.broadcasted_iota(
        jnp.int32, (rows, vhead), 1
    )
    line = lax.broadcasted_iota(jnp.int32, (8, vhead), 0)
    token = lax.broadcasted_iota(jnp.int32, (rows, tokens), 1)

    for t in range(trips):
        pool_part(t).wait()
        ns = [t * group + k for k in range(group)]
        scores = [
            lax.dot_general(
                query_ref[n],
                pool_ref[in_turn(n)],
                (((1,), (1,)), ((), ())),
                preferred_element_type=F32,
            )
            * scale
            for n in ns
        ]
        scores = [jnp.where(token < live_ref[in_turn(n)], x, NEG_FILL) for n, x in zip(ns, scores)]
        tops = [jnp.max(x, axis=1, keepdims=True) for x in scores]
        weights = [jnp.exp(x - top) for x, top in zip(scores, tops)]
        totals = [jnp.sum(x, axis=1, keepdims=True) for x in weights]
        weighted = [
            jnp.dot(x.astype(BF16), pool_ref[in_turn(n), :, :latent], preferred_element_type=F32)
            for n, x in zip(ns, weights)
        ]
        for n, top, total, x in zip(ns, tops, totals, weighted):
            mean_ref[n] = (x * (1.0 / total)).astype(BF16)
            mass = jnp.sum(jnp.where(eye, top + jnp.log(total), 0.0), axis=0, keepdims=True)
            high = mass.astype(BF16).astype(F32)
            middle = (mass - high).astype(BF16).astype(F32)
            low = mass - high - middle
            parts = jnp.where(line == 0, high, jnp.where(line == 1, middle, low))
            out_ref[n, rows:, :] = jnp.where(line < PARTS, parts, 0.0).astype(BF16)
        if t % 2 == 1:
            if t == 1:
                values_copy.wait()
            project((t - 1) * group, 2 * group)
            leaving(t - 1).start()
            leaving(t).start()
    for t in range(trips):
        leaving(t).wait()


def lend(live, arrived, key_absorb, value_absorb, pool, scale, group=8):
    slots, _, width = pool.shape
    latent = key_absorb.shape[2]
    vhead = value_absorb.shape[-1]
    rows = arrived.shape[1] * 2 // 3
    vmem = pl.BlockSpec(memory_space=pltpu.VMEM)
    hbm = pl.BlockSpec(memory_space=pl.ANY)
    return pl.pallas_call(
        functools.partial(lend_kernel, scale, group),
        out_shape=pltpu.HBM((slots, rows + 8, vhead), BF16),
        in_specs=[pl.BlockSpec(memory_space=pltpu.SMEM), vmem, vmem, hbm, hbm],
        out_specs=pl.BlockSpec(memory_space=pltpu.HBM),
        scratch_shapes=[
            pltpu.VMEM((slots, rows + 8, vhead), BF16),
            pltpu.VMEM(value_absorb.shape, BF16),
            pltpu.VMEM(pool.shape, BF16),
            pltpu.VMEM((slots, rows, width), BF16),
            pltpu.VMEM((slots, rows, latent), BF16),
            pltpu.SemaphoreType.DMA((2 * (slots // group) + 1,)),
        ],
        compiler_params=pltpu.CompilerParams(vmem_limit_bytes=28 * 2**20),
        name="lend",
    )(
        live,
        arrived,
        key_absorb,
        pltpu.with_memory_space_constraint(value_absorb, pltpu.HBM),
        pltpu.with_memory_space_constraint(pool, pltpu.HBM),
    )


def settle_kernel(back_ref, local_ref, draft_scores_ref, draft_values_ref, out_ref, rows_ref, wide_ref):
    slots, _, vhead = back_ref.shape
    reqs, rows, drafts = draft_scores_ref.shape
    heads = rows // drafts
    mass = jnp.sum(back_ref[:, rows:, :].astype(F32), axis=1)
    mass = jnp.transpose(mass)[:rows]
    local = local_ref[...]
    for i in range(reqs):
        member = local == i
        draft = draft_scores_ref[i]
        own = jnp.where(member, mass, NEG_FILL)
        top = jnp.maximum(
            jnp.max(own, axis=1, keepdims=True), jnp.max(draft, axis=1, keepdims=True)
        )
        weight = jnp.where(member, jnp.exp(own - top), 0.0)
        draft = jnp.exp(draft - top)
        total = jnp.sum(weight, axis=1, keepdims=True) + jnp.sum(draft, axis=1, keepdims=True)
        value = jnp.zeros((rows, vhead), F32)
        for n in range(slots):
            value = value + weight[:, n : n + 1] * back_ref[n, :rows, :].astype(F32)
        for j in range(drafts):
            for s in range(drafts):
                wide_ref[pl.ds(j * rows + s, heads, stride=drafts), :] = draft_values_ref[i, j]
            value = value + draft[:, j : j + 1] * wide_ref[j * rows : (j + 1) * rows]
        value = value / total
        for h in range(heads):
            at = (h * reqs + i) * drafts
            rows_ref[at : at + drafts, :] = value[h * drafts : (h + 1) * drafts]
    size = reqs * drafts
    joined = jnp.concatenate([rows_ref[h * size : (h + 1) * size] for h in range(heads)], 1)
    joined = joined.astype(BF16)
    for n in range(out_ref.shape[0]):
        out_ref[n] = joined


def settle(back, local, draft_scores, draft_values, copies):
    _, _, vhead = back.shape
    reqs, rows, drafts = draft_scores.shape
    vmem = pl.BlockSpec(memory_space=pltpu.VMEM)
    return pl.pallas_call(
        settle_kernel,
        out_shape=jax.ShapeDtypeStruct((copies, reqs * drafts, rows // drafts * vhead), BF16),
        in_specs=[vmem] * 4,
        out_specs=vmem,
        scratch_shapes=[
            pltpu.VMEM((reqs * rows, vhead), F32),
            pltpu.VMEM((drafts * rows, vhead), F32),
        ],
        compiler_params=pltpu.CompilerParams(vmem_limit_bytes=8 * 2**20),
        name="settle",
    )(back, local, draft_scores, draft_values)


def mix_kernel(place_ref, rows_ref, *refs):
    weights, (own_ref, other_ref, late_ref, held_ref, sems) = refs[:-5], refs[-5:]
    blocks = held_ref.shape[0]
    late = {
        k: pltpu.make_async_copy(weights[k], late_ref.at[n], sems.at[n])
        for n, k in enumerate((1, 2))
    }
    for copy in late.values():
        copy.start()
    dot = functools.partial(
        lax.dot_general,
        dimension_numbers=(((1,), (1,)), ((), ())),
        preferred_element_type=F32,
    )
    for k in (0, 3, 1, 2):
        if k in late:
            late[k].wait()
        done = dot(rows_ref[...], late_ref[k - 1] if k in late else weights[k][...])
        held_ref[k] = done
    for n in range(blocks):
        out_ref = (own_ref, other_ref)[n * 2 // blocks]
        piece = held_ref[place_ref[n]]
        size = piece.shape[0] // len(TURN)
        places = [TURN.index(z) * size for z in range(len(TURN))]
        piece = jnp.concatenate([piece[at : at + size] for at in places])
        out_ref[n % (blocks // 2)] = piece.reshape(out_ref.shape[1:]).astype(BF16)


def mix(place, rows, weights, drafts):
    blocks = place.shape[0]
    features = weights[0].shape[0]
    vmem = pl.BlockSpec(memory_space=pltpu.VMEM)
    half = jax.ShapeDtypeStruct((blocks // 2, rows.shape[0] // drafts, drafts, features), BF16)
    return pl.pallas_call(
        mix_kernel,
        out_shape=[half, half],
        in_specs=[
            pl.BlockSpec(memory_space=pltpu.SMEM),
            vmem,
            *[pl.BlockSpec(memory_space=pl.ANY) if i in (1, 2) else vmem for i in range(blocks)],
        ],
        out_specs=[vmem, vmem],
        scratch_shapes=[
            pltpu.VMEM((2,) + weights[0].shape, BF16),
            pltpu.VMEM((blocks, rows.shape[0], features), F32),
            pltpu.SemaphoreType.DMA((2,)),
        ],
        compiler_params=pltpu.CompilerParams(vmem_limit_bytes=12 * 2**20),
        name="mix",
    )(place, rows, *weights)


def body(
    draft_queries,
    draft_latents,
    latent_pool,
    key_absorb,
    value_absorb,
    out_proj,
    slot_request,
    context_lengths,
):
    home = lax.axis_index("lender")
    reqs, drafts, heads, width = draft_queries.shape
    nope, latent = key_absorb.shape[1:]
    tokens = latent_pool.shape[1]
    rows = heads * drafts
    scale = width ** (-0.5) * MSCALE_SQ

    outgoing = pack(jnp.full((1,), home, jnp.int32), slot_request, draft_queries, nope)
    outgoing, slot_request, context_lengths, draft_queries, draft_latents, out_proj = (
        lax.optimization_barrier(
            (outgoing, slot_request, context_lengths, draft_queries, draft_latents, out_proj)
        )
    )
    slots = latent_pool.shape[0]
    turn = [in_turn(n) for n in range(slots)]
    arrived = lax.all_to_all(
        outgoing, "lender", split_axis=0, concat_axis=0, tiled=True, axis_index_groups=[turn]
    )

    live_all = live_tokens(slot_request, context_lengths, tokens)
    live_here = lax.dynamic_slice_in_dim(live_all, home, 1, 0)[0]
    local = lax.dynamic_slice_in_dim(slot_request, home, 1, 1)[:, 0] - home * reqs
    local = local.reshape(-1, len(TURN))
    local = jnp.stack([local[:, z] for z in TURN], axis=1).reshape(1, -1)
    lenders, column = latent_pool.shape[0], 8
    planes = lenders // column
    up = [(l, (l - column) % lenders) for l in range(lenders)]
    down = [(l, (l + column) % lenders) for l in range(lenders)]
    weight = out_proj.T
    weight_up = lax.ppermute(weight, "lender", up)

    part = jnp.einsum(
        "ishc,hcl->ihsl", draft_queries[..., :nope], key_absorb, preferred_element_type=F32
    ).astype(BF16)
    own = jnp.concatenate([part, jnp.swapaxes(draft_queries[..., nope:], 1, 2)], -1)
    draft_scores = (
        jnp.einsum("ihsk,ijk->ihsj", own, draft_latents, preferred_element_type=F32) * scale
    )
    causal = jnp.arange(drafts)[:, None] >= jnp.arange(drafts)[None, :]
    draft_scores = jnp.where(causal, draft_scores, NEG_FILL).reshape(reqs, rows, drafts)
    draft_values = jnp.einsum(
        "ijl,hlc->ijhc", draft_latents[:, :, :latent], value_absorb, preferred_element_type=F32
    )
    arrived, live_here, local, draft_scores, draft_values = lax.optimization_barrier(
        (arrived, live_here, local, draft_scores, draft_values)
    )

    sending = lend(live_here, arrived, key_absorb, value_absorb, latent_pool, scale)
    sending, weight = lax.optimization_barrier((sending, weight))
    back = lax.all_to_all(
        sending, "lender", split_axis=0, concat_axis=0, tiled=True, axis_index_groups=[turn]
    )
    weight_far = lax.ppermute(weight_up, "lender", up)
    weight_down = lax.ppermute(weight, "lender", down)

    copies = settle(back, local, draft_scores, draft_values, column)
    inner = [[in_turn(column * y + z) for z in range(column)] for y in range(planes)]
    plane = lax.all_to_all(
        copies, "lender", split_axis=0, concat_axis=0, tiled=True, axis_index_groups=inner
    )
    plane, weight_far, weight_down = lax.optimization_barrier((plane, weight_far, weight_down))
    y = home // column
    tensor = lax.axis_index("tensor")
    x, core = tensor // 2, tensor % 2
    turns = [core, core + 2, 1 - core, 3 - core]
    place = jnp.stack([(x + k - y) % planes for k in turns]).astype(jnp.int32)
    weight_up, weight_far = (
        pltpu.with_memory_space_constraint(w, pltpu.HBM) for w in (weight_up, weight_far)
    )
    weights = [weight, weight_up, weight_far, weight_down]
    own, other = mix(place, plane.reshape(-1, plane.shape[-1]), weights, drafts)

    tensors = lax.axis_size("tensor")
    swap = [(t, t ^ 1) for t in range(tensors)]
    own = (own.astype(F32) + lax.ppermute(other, "tensor", swap).astype(F32)).astype(BF16)
    total = None
    for j in range(planes // 2):
        pairs = []
        for index in range(lenders * tensors):
            (source_y, z), source = divmod(index // tensors, column), index % tensors
            lender = (source // 2 + source % 2 + 2 * j) % planes * column + z
            pairs.append((index, lender * tensors + source_y * 2 + source % 2))
        piece = lax.ppermute(own[j], ("lender", "tensor"), pairs).astype(F32)
        total = piece if total is None else total + piece
    half = total.shape[0] // 2
    mine = jnp.where(core == 0, total[:half], total[half:])
    theirs = jnp.where(core == 0, total[half:], total[:half])
    return (mine + lax.ppermute(theirs, "tensor", swap)).astype(BF16)


def solution(mesh):
    in_specs = (
        P("lender", None, "tensor", None),
        P("lender", None, None),
        P("lender", None, None),
        P("tensor", None, None),
        P("tensor", None, None),
        P("tensor", "lender"),
        P(),
        P(),
    )
    out_specs = P("tensor", None, "lender")
    return jax.shard_map(body, mesh=mesh, in_specs=in_specs, out_specs=out_specs, check_vma=False)
```
